128 devices in a mesh: dp: 16 (over x, y), expert: 8 (over z, core).
Axes of the slice: x: 4, y: 4, z: 4, core: 2. Of those that a mesh axis runs over, the one named last changes fastest.
Arguments:
- tokens: bfloat16 [16384, 1536], P(('dp', 'expert')), may hold values from -6 to 6
- norm_attn: float32 [1536], replicated, may hold values from 0.5 to 1.5
- query_weight: bfloat16 [1536, 1536], P('dp'), may hold values from -0.15625 to 0.15625
- key_weight: bfloat16 [1536, 512], P('dp'), may hold values from -0.15625 to 0.15625
- value_weight: bfloat16 [1536, 512], P('dp'), may hold values from -0.15625 to 0.15625
- out_weight: bfloat16 [1536, 1536], P('dp'), may hold values from -0.625 to 0.625
- norm_moe: float32 [1536], replicated, may hold values from 0.5 to 1.5
- router_weight: bfloat16 [1536, 24], P('dp'), may hold values from -0.078125 to 0.078125
- gate_weight: bfloat16 [24, 1536, 512], P('expert'), may hold values from -0.15625 to 0.15625
- up_weight: bfloat16 [24, 1536, 512], P('expert'), may hold values from -0.15625 to 0.15625
- down_weight: bfloat16 [24, 512, 1536], P('expert'), may hold values from -2 to 2
- routes: int32 [16384, 8], P(('dp', 'expert')), may hold values from 0 to 23, all different within a row; in each aligned block of 128 rows (0 to 127, 128 to 255, ...) at most 56 rows name the same one
- seq_lengths: int32 [16, 3], P('dp'), may hold values from 1 to 1022, as said below
- out_grad: bfloat16 [16384, 1536], P(('dp', 'expert')), may hold values from -6 to 6
Outputs:
- layer_out: bfloat16 [16384, 1536], P(('dp', 'expert'))
- input_grad: bfloat16 [16384, 1536], P(('dp', 'expert'))
- norm_attn_grad: float32 [1536], replicated
- query_grad: float32 [1536, 1536], P('dp')
- key_grad: float32 [1536, 512], P('dp')
- value_grad: float32 [1536, 512], P('dp')
- out_weight_grad: float32 [1536, 1536], P('dp')
- norm_moe_grad: float32 [1536], replicated
- router_grad: float32 [1536, 24], P('dp')
- gate_grad: float32 [24, 1536, 512], P('expert')
- up_grad: float32 [24, 1536, 512], P('expert')
- down_grad: float32 [24, 512, 1536], P('expert')
The draws below stay inside these ranges and needn't reach their ends.
Inputs may be any that keep to these rules, and one draw needn't show every extreme that they name: `routes`: in each aligned block of 128 rows (the rows of one device) the 8 experts of a row differ, and no expert is named by more than 56 rows. `seq_lengths`: each row sums to 1024; in each row one sequence, at a place drawn from the seed, starts among the group's first 128 tokens and ends among its last 128; in some row it has 1022 tokens.
All inputs are finite; a program needn't handle non-finite values.
Results may differ from the reference program's by a relative error of at most 0.025.
Values may be sent and summed in bfloat16 or wider, within the bound.
No kernel may reach another device: no remote copies, remote signals or barrier semaphores. Data moves between devices by JAX's collectives and lax.ppermute only.
A program may use at most 192 MiB of HBM per device.

```python
import math
import jax
import jax.numpy as jnp
import numpy as np
from jax import lax

D = 1536
QH = 24
KVH = 8
HD = 64
FFE = 512
TOP = 8
EXP_DEV = 3
SEQS = 3
TOK_DEV = 128
EXPERTS = 24
CAP = 56
TOKENS = 16384
N_DP = 16
N_EXPERT = 8


def draw_seq_lengths(key, part):
    key = jax.random.fold_in(key, 11)
    group_rows = TOK_DEV * N_EXPERT
    short_most = max(TOK_DEV // 2 - 1, 1)
    key_short, key_place, key_group = jax.random.split(key, 3)
    shorts = jax.random.randint(key_short, (N_DP, SEQS - 1), 1, short_most + 1, dtype=jnp.int32)
    chosen = jax.random.randint(key_group, (), 0, N_DP, dtype=jnp.int32)
    group_index = jnp.arange(N_DP, dtype=jnp.int32)[:, None]
    shorts = jnp.where(group_index == chosen, 1, shorts).astype(jnp.int32)
    longest = group_rows - jnp.sum(shorts, axis=1, keepdims=True).astype(jnp.int32)
    place = jax.random.randint(key_place, (N_DP, 1), 0, SEQS, dtype=jnp.int32)
    column = jnp.arange(SEQS, dtype=jnp.int32)[None, :]
    short_index = jnp.clip(column - (column > place).astype(jnp.int32), 0, SEQS - 2)
    picked = jnp.take_along_axis(shorts, short_index, axis=1)
    return jnp.where(column == place, longest, picked).astype(jnp.int32)


def level_of(rng, dims, cuts, low, top_value):
    def one(axis_at, shards_of):
        heights = jax.random.uniform(jax.random.fold_in(jax.random.fold_in(rng, 6), axis_at), (shards_of,), jnp.float32, low / len(cuts), top_value / len(cuts))
        return jnp.repeat(jnp.exp(heights), dims[axis_at] // shards_of).reshape((-1,) + (1,) * (len(dims) - axis_at - 1))

    factor_of = one(*cuts[0])
    for cut in cuts[1:]:
        factor_of = factor_of * one(*cut)
    return factor_of


def shared_out(own_key, own, number, rows, number_of, top, bound, skew):
    order = jax.random.permutation(own_key, number_of)
    crowded, common = portions_of(number_of, rows * top, bound, skew, True), portions_of(number_of, rows * top, bound, skew, False)
    places = jnp.arange(number_of)

    def named(tallies, rotation):
        used = int((tallies > 0).sum())
        fixed = max(1, used // 4)
        shifted = fixed + (places - fixed + rotation * (used - fixed)) % max(1, number_of - fixed)
        return jnp.zeros((number_of,), jnp.int32).at[order[jnp.where(places < fixed, places, shifted)]].set(jnp.asarray(tallies, jnp.int32))

    tallies = jnp.where(number % 4 == 0, named(crowded, number // 4), named(common, number - number // 4 - 1))
    mixed = jax.random.permutation(jax.random.fold_in(own, 3), number_of)
    donor, taker = mixed[0:number_of // 2 * 2:2], mixed[1:number_of // 2 * 2:2]
    slack = jnp.minimum(tallies[donor] - 1, bound - tallies[taker]) // 2
    slack = jnp.where((donor == order[0]) | (taker == order[0]) | (tallies[taker] == 0), 0, jnp.maximum(slack, 0))
    shifted = jax.random.randint(jax.random.fold_in(own, 4), (number_of // 2,), 0, 1 << 20) % (slack + 1)
    tallies = tallies.at[donor].add(-shifted).at[taker].add(shifted)
    members = jnp.searchsorted(jnp.cumsum(tallies), jnp.arange(rows * top), side="right").astype(jnp.int32)
    table = members.reshape(top, rows).T
    table = table[jax.random.permutation(jax.random.fold_in(own, 1), rows)]
    rotation = jax.random.randint(jax.random.fold_in(own, 2), (rows, 1), 0, top)
    return jnp.take_along_axis(table, (jnp.arange(top)[None, :] + rotation) % top, axis=1)


def portions_of(count, total, most, slope, full):
    portions = [(1 << 20) // math.isqrt(grade ** slope) + 1 for grade in range(1, count + 1)]
    largest = most if full else min(most, max(-(-total // count), total * portions[0] // sum(portions)))
    least = 1 if total - largest >= count - 1 else 0
    counts, spare = [largest] + [least] * (count - 1), total - largest - least * (count - 1)
    while spare > 0:
        candidates = [i for i in range(1, count) if counts[i] < largest] or [i for i in range(1, count) if counts[i] < most]
        pool, budget = sum([portions[i] for i in candidates]), spare
        for i in candidates:
            more = min(most - counts[i], max(1, budget * portions[i] // pool), spare)
            counts[i] = counts[i] + more
            spare = spare - more
    return np.array(counts)


def centred(own_key, extent, scale, most, cuts=(), kind=jnp.bfloat16):
    drawn = scale * jax.random.normal(own_key, extent, jnp.float32)
    if cuts:
        drawn = drawn * level_of(own_key, extent, cuts, -0.22, 0.18)
    return jnp.clip(drawn, -most, most).astype(kind)


def setup_inputs(seed: int = 0) -> dict:
    splits = jax.random.split(jax.random.key(seed), 15)
    tokens = centred(splits[0], (TOKENS, D), 1.0, 6.0, ((0, 128),))
    norm_attn = jnp.clip(1.0 + 0.1 * jax.random.normal(splits[1], (D,), jnp.float32), 0.5, 1.5)
    query_weight = centred(splits[2], (D, QH * HD), D ** -0.5, 0.15625, ((0, 16),))
    key_weight = centred(splits[3], (D, KVH * HD), D ** -0.5, 0.15625, ((0, 16),))
    value_weight = centred(splits[4], (D, KVH * HD), D ** -0.5, 0.15625, ((0, 16),))
    out_weight = centred(splits[5], (QH * HD, D), (max(QH * HD // 16, 1)) ** -0.5, 0.625, ((0, 16),))
    norm_moe = jnp.clip(1.0 + 0.1 * jax.random.normal(splits[6], (D,), jnp.float32), 0.5, 1.5)
    router_weight = centred(splits[7], (D, EXPERTS), (4 * D) ** -0.5, 0.078125, ((0, 16),))
    gate_weight = centred(splits[8], (EXPERTS, D, FFE), D ** -0.5, 0.15625, ((0, 8),))
    up_weight = centred(splits[9], (EXPERTS, D, FFE), D ** -0.5, 0.15625, ((0, 8),))
    down_weight = centred(splits[10], (EXPERTS, FFE, D), (max(FFE // 64, 1)) ** -0.5, 2.0, ((0, 8),))
    routes_keys = jax.random.split(jax.random.fold_in(splits[11], 1), TOKENS // TOK_DEV)
    routes_turns = jax.random.permutation(jax.random.fold_in(splits[11], 3), TOKENS // TOK_DEV)
    routes = jax.vmap(lambda own, number: shared_out(jax.random.fold_in(splits[11], 2), own, number, TOK_DEV, EXPERTS, TOP, CAP, 1))(routes_keys, routes_turns).reshape((TOKENS, TOP))
    seq_lengths = draw_seq_lengths(jax.random.fold_in(splits[14], 71), 0)
    out_grad = centred(splits[13], (TOKENS, D), 1.0, 6.0, ((0, 128),))
    return dict(tokens=tokens, norm_attn=norm_attn, query_weight=query_weight, key_weight=key_weight, value_weight=value_weight, out_weight=out_weight, norm_moe=norm_moe, router_weight=router_weight, gate_weight=gate_weight, up_weight=up_weight, down_weight=down_weight, routes=routes, seq_lengths=seq_lengths, out_grad=out_grad)


@jax.custom_vjp
def low(v):
    return lax.optimization_barrier(v.astype(jnp.bfloat16)).astype(jnp.float32)

@jax.custom_vjp
def low_back(v):
    return v

def low_keep(v):
    return (low(v), None)

def low_pass(kept, grad):
    return (grad,)

def back_keep(v):
    return (v, None)

def back_low(kept, grad):
    return (low(grad),)
low.defvjp(low_keep, low_pass)
low_back.defvjp(back_keep, back_low)
EPS = 1e-06
THETA = 10000.0
HIGHEST_PREC = lax.Precision.HIGHEST

def matmul(left, right):
    return jnp.dot(left, right, precision=HIGHEST_PREC)

def rms_norm(values, gain):
    return values * lax.rsqrt(lax.optimization_barrier(jnp.mean(values * values, axis=-1, keepdims=True)) + EPS) * gain

def rotate(values, cos_table, sin_table):
    half = values.shape[-1] // 2
    first_half = values[..., :half]
    second_half = values[..., half:]
    return jnp.concatenate([first_half * cos_table - second_half * sin_table, second_half * cos_table + first_half * sin_table], axis=-1)

def sequence_table(seq_row, count):
    ends = jnp.cumsum(seq_row).astype(jnp.int32)
    starts = (ends - seq_row).astype(jnp.int32)
    where_all = jnp.arange(count, dtype=jnp.int32)
    seg_ids = lax.optimization_barrier(jnp.sum((where_all[:, None] >= ends[None, :]).astype(jnp.int32), axis=1)).astype(jnp.int32)
    seq_index = jnp.arange(seq_row.shape[0], dtype=jnp.int32)
    first_of = lax.optimization_barrier(jnp.sum(jnp.where(seg_ids[:, None] == seq_index[None, :], starts[None, :], 0), axis=1)).astype(jnp.int32)
    return (seg_ids, (where_all - first_of).astype(jnp.int32))

def angle_tables(positions, head_size):
    steps_f = jnp.arange(head_size // 2, dtype=jnp.float32)
    freq = jnp.exp(steps_f * (-2.0 * math.log(THETA) / head_size))
    angles = positions.astype(jnp.float32)[:, None] * freq[None, :]
    return (jnp.cos(angles)[:, None, :], jnp.sin(angles)[:, None, :])

def dispatch_table(route_g, experts, slot_cap, owners, tok_rows):
    per_dev = route_g.reshape(owners, tok_rows * TOP)
    one_hot = (per_dev[:, :, None] == jnp.arange(experts, dtype=jnp.int32)[None, None, :]).astype(jnp.int32)
    slot_ranks = (lax.optimization_barrier(jnp.sum(jnp.cumsum(one_hot, axis=1).astype(jnp.int32) * one_hot, axis=2)) - 1).astype(jnp.int32)
    column = (jnp.arange(owners, dtype=jnp.int32)[:, None] * slot_cap + slot_ranks).astype(jnp.int32)
    slot_ids = jnp.arange(owners * tok_rows * TOP, dtype=jnp.int32)
    empty = jnp.full((experts, owners * slot_cap), owners * tok_rows * TOP, jnp.int32)
    return empty.at[per_dev.reshape(-1), column.reshape(-1)].set(slot_ids)

def layer_forward(x_in, weights, allowed, cos_table, sin_table, route_g, slot_table):
    gain_one, w_query, w_key, w_value, w_out, gain_two, w_router, w_gate, w_up, w_down = weights
    group_rows = x_in.shape[0]
    head_ratio = QH // KVH
    score_scale = 1.0 / math.sqrt(HD)
    normed_one = low(rms_norm(x_in, gain_one))
    query = low(rotate(low_back(matmul(normed_one, w_query)).reshape(group_rows, QH, HD), cos_table, sin_table))
    key = low(rotate(low_back(matmul(normed_one, w_key)).reshape(group_rows, KVH, HD), cos_table, sin_table))
    value = low(low_back(matmul(normed_one, w_value))).reshape(group_rows, KVH, HD)
    q_heads = jnp.moveaxis(query.reshape(group_rows, KVH, head_ratio, HD), 1, 0)
    k_heads = jnp.moveaxis(key, 1, 0)
    v_heads = jnp.moveaxis(value, 1, 0)

    def attend(head_block):
        q_h, k_h, v_h = head_block
        scores = low_back(jnp.einsum('qrd,kd->rqk', q_h, k_h, precision=HIGHEST_PREC) * score_scale)
        scores = jnp.where(allowed[None], scores, -1e+30)
        row_top = lax.optimization_barrier(jnp.max(scores, axis=-1, keepdims=True))
        exp_terms = jnp.exp(scores - row_top)
        prob_low = low(exp_terms / lax.optimization_barrier(jnp.sum(exp_terms, axis=-1, keepdims=True)))
        return jnp.einsum('rqk,kd->qrd', prob_low, v_h, precision=HIGHEST_PREC)
    mixed = lax.map(jax.checkpoint(attend), (q_heads, k_heads, v_heads))
    attn_out = low(low_back(jnp.moveaxis(mixed, 0, 1).reshape(group_rows, QH * HD)))
    hidden = x_in + low_back(matmul(attn_out, w_out))
    normed_two = low(rms_norm(hidden, gain_two))
    logits = matmul(normed_two, w_router)
    logit_top = lax.optimization_barrier(jnp.max(logits, axis=-1, keepdims=True))
    logit_exp = jnp.exp(logits - logit_top)
    router_prob = logit_exp / lax.optimization_barrier(jnp.sum(logit_exp, axis=-1, keepdims=True))
    gate_vals = jnp.take_along_axis(router_prob, route_g, axis=1)
    width = x_in.shape[1]
    slot_rows = low_back(jnp.broadcast_to(normed_two[:, None, :], (group_rows, TOP, width)).reshape(group_rows * TOP, width))
    padded = jnp.concatenate([slot_rows, jnp.zeros((1, width), jnp.float32)], axis=0)
    expert_rows = padded[slot_table]
    gate_in = low_back(jnp.einsum('emd,edf->emf', expert_rows, w_gate, precision=HIGHEST_PREC))
    up_in = low_back(jnp.einsum('emd,edf->emf', expert_rows, w_up, precision=HIGHEST_PREC))
    inner_act = low(jax.nn.silu(gate_in) * up_in)
    expert_out = low(low_back(jnp.einsum('emf,efd->emd', inner_act, w_down, precision=HIGHEST_PREC)))
    slot_out = jnp.zeros((group_rows * TOP + 1, width), jnp.float32).at[slot_table.reshape(-1)].add(expert_out.reshape(-1, width))
    per_slot = slot_out[:group_rows * TOP].reshape(group_rows, TOP, width)
    mixture = lax.optimization_barrier(jnp.sum(gate_vals[:, :, None] * per_slot, axis=1))
    return hidden + mixture

def reference(tokens, norm_attn, query_weight, key_weight, value_weight, out_weight, norm_moe, router_weight, gate_weight, up_weight, down_weight, routes, seq_lengths, out_grad):
    group_rows = TOK_DEV * N_EXPERT
    experts = EXP_DEV * N_EXPERT
    slot_cap = min(TOK_DEV, TOK_DEV * TOP * 4 // (experts * 3))
    params = (norm_attn.astype(jnp.float32), query_weight.astype(jnp.float32), key_weight.astype(jnp.float32), value_weight.astype(jnp.float32), out_weight.astype(jnp.float32), norm_moe.astype(jnp.float32), router_weight.astype(jnp.float32), gate_weight.astype(jnp.float32), up_weight.astype(jnp.float32), down_weight.astype(jnp.float32))
    width = tokens.shape[1]
    x_groups = tokens.astype(jnp.float32).reshape(N_DP, group_rows, width)
    dy_groups = out_grad.astype(jnp.float32).reshape(N_DP, group_rows, width)
    route_groups = routes.reshape(N_DP, group_rows, TOP)

    def one_group(grad_sums, inputs):
        x_g, dy_g, route_g, len_g = inputs
        seg_ids, positions = sequence_table(len_g, group_rows)
        where_all = jnp.arange(group_rows, dtype=jnp.int32)
        allowed = (seg_ids[:, None] == seg_ids[None, :]) & (where_all[None, :] <= where_all[:, None])
        cos_table, sin_table = angle_tables(positions, HD)
        slot_table = dispatch_table(route_g, experts, slot_cap, N_EXPERT, TOK_DEV)

        def forward_of(x_in, weights):
            return layer_forward(x_in, weights, allowed, cos_table, sin_table, route_g, slot_table)
        y_g, pull = jax.vjp(forward_of, x_g, params)
        x_grad, w_grads = pull(dy_g)
        new_sums = tuple((s + g for s, g in zip(grad_sums, w_grads)))
        return (new_sums, (y_g, x_grad))
    zero_sums = tuple((jnp.zeros_like(p) for p in params))
    grad_sums, (y_all, dx_all) = lax.scan(one_group, zero_sums, (x_groups, dy_groups, route_groups, seq_lengths))
    layer_out = y_all.reshape(-1, width).astype(jnp.bfloat16)
    input_grad = dx_all.reshape(-1, width).astype(jnp.bfloat16)
    return (layer_out, input_grad, grad_sums[0], grad_sums[1], grad_sums[2], grad_sums[3], grad_sums[4], grad_sums[5], grad_sums[6], grad_sums[7], grad_sums[8], grad_sums[9])
```

```python
import functools
import math

import jax
import jax.numpy as jnp
from jax import lax
from jax.experimental import pallas as pl
from jax.experimental.pallas import tpu as pltpu
from jax.sharding import PartitionSpec as P

QH = 24
KVH = 8
HD = 64
TOP = 8
EXP_DEV = 3
CAP = 56
D = 1536
FFE = 512
ROWS = 128
OWN = 8
GROUP = 1024
DP = 16
EXPERTS = 24
HEADS = 3
QW = HEADS * HD
PAIR = 2 * CAP
PAIRS = OWN // 2
SLOTS = OWN * CAP
BLK = 256
WW = 384
XW = D + 128
EPS = 1e-06
THETA = 10000.0
VMEM = 60 * 1024 * 1024
f32 = jnp.float32
bf16 = jnp.bfloat16

NN = (((1,), (0,)), ((), ()))
NT = (((1,), (1,)), ((), ()))
TN = (((0,), (0,)), ((), ()))


def mm(a, b, dims=NN):
    return lax.dot_general(a, b, dims, preferred_element_type=f32)


def iota(shape, dim):
    return lax.broadcasted_iota(jnp.int32, shape, dim)


def swap_halves(v):
    lane = iota(v.shape, 1) % HD
    width = v.shape[1]
    ahead = pltpu.roll(v, width - HD // 2, 1)
    behind = pltpu.roll(v, HD // 2, 1)
    return jnp.where(lane < HD // 2, ahead, behind)


def block_mask(start_ref, at, keys):
    place = at + iota((BLK, keys), 0)
    key = iota((BLK, keys), 1)
    first = start_ref[pl.ds(at, BLK), :]
    return (key <= place) & (key >= first)


def attend_kernel(x_ref, w_ref, gain_ref, cos_ref, sin_ref, start_ref, normed_ref, qkv_ref, mix_ref, log_ref):
    for at in range(0, GROUP, BLK):
        rows = pl.ds(at, BLK)
        x = x_ref[rows, :].astype(f32)
        scale = lax.rsqrt(jnp.mean(x * x, axis=-1, keepdims=True) + EPS)
        normed = (x * scale * gain_ref[...]).astype(bf16)
        normed_ref[rows, :] = normed
        raw = mm(normed, w_ref[...])
        turned = raw[:, :BLK]
        turned = turned * cos_ref[rows, :] + swap_halves(turned) * sin_ref[rows, :]
        qkv_ref[rows, 0:BLK] = turned.astype(bf16)
        qkv_ref[rows, BLK:WW] = raw[:, BLK:WW].astype(bf16)
    for at in range(0, GROUP, BLK):
        rows = pl.ds(at, BLK)
        keys = at + BLK
        seen = block_mask(start_ref, at, keys)
        k_h = qkv_ref[0:keys, QW : QW + HD]
        v_h = qkv_ref[0:keys, BLK : BLK + HD]
        for r in range(HEADS):
            q_h = qkv_ref[rows, r * HD : (r + 1) * HD] * jnp.asarray(HD**-0.5, bf16)
            scores = jnp.where(seen, mm(q_h, k_h, NT), -1e30)
            top = jnp.max(scores, axis=-1, keepdims=True)
            terms = jnp.exp(scores - top)
            total = jnp.sum(terms, axis=-1, keepdims=True)
            prob = (terms / total).astype(bf16)
            mix_ref[rows, r * HD : (r + 1) * HD] = mm(prob, v_h).astype(bf16)
            log_ref[rows, r : r + 1] = top + jnp.log(total)


def out_kernel(mix_ref, wo_ref, x_ref, gain_ref, hidden_ref, normed_ref):
    hidden = x_ref[...].astype(f32)
    for j in range(OWN):
        hidden = hidden + mm(mix_ref[j], wo_ref[j * QW : (j + 1) * QW, :])
    hidden_ref[...] = hidden
    scale = lax.rsqrt(jnp.mean(hidden * hidden, axis=-1, keepdims=True) + EPS)
    normed_ref[...] = (hidden * scale * gain_ref[...]).astype(bf16)


def router_probs(normed, w_ref):
    logits = mm(normed, w_ref[:, BLK:WW])
    lane = iota(logits.shape, 1)
    real = (lane >= HD) & (lane < HD + EXPERTS)
    logits = jnp.where(real, logits, -1e30)
    terms = jnp.exp(logits - jnp.max(logits, axis=-1, keepdims=True))
    terms = jnp.where(real, terms, 0.0)
    return terms / jnp.sum(terms, axis=-1, keepdims=True)


def pick_rows(slot_row, b):
    row = slot_row[:, b * BLK : (b + 1) * BLK]
    return iota((PAIR, BLK), 0) == row


def expert_kernel(
    own_ref, n_ref, dy_ref, routes_ref, w_ref, wg_ref, wu_ref, wd_ref,
    gg_ref, gu_ref, gd_ref, hg_ref, hu_ref, gated_ref, p_ref, slot_ref,
    prob_ref, x_ref, d_ref, gate_ref,
):
    e = pl.program_id(0)
    own = own_ref[0] * EXP_DEV + e

    @pl.when(e == 0)
    def _():
        for at in range(0, GROUP, BLK):
            probs = router_probs(n_ref[at : at + BLK, :], w_ref)
            prob_ref[:, at : at + BLK] = jnp.transpose(probs)

    chosen = jnp.max((routes_ref[...] == own).astype(f32), axis=0, keepdims=True)
    gate_row = jnp.sum(jnp.where(iota((128, GROUP), 0) == HD + own, prob_ref[...], 0.0), axis=0, keepdims=True)
    before = (iota((ROWS, ROWS), 0) < iota((ROWS, ROWS), 1)).astype(f32).astype(bf16)
    ranks = []
    for s in range(OWN):
        part = jnp.broadcast_to(chosen[:, s * ROWS : (s + 1) * ROWS], (8, ROWS)).astype(bf16)
        ranks.append(mm(part, before)[0:1] + float(CAP * (s % 2)))
    rank = jnp.concatenate(ranks, axis=1)
    slot_row = jnp.where(chosen > 0.0, rank, -1.0).astype(jnp.int32)
    slot_ref[0] = jnp.broadcast_to(slot_row, (8, GROUP))
    for b in range(PAIRS):
        pick = pick_rows(slot_row, b)
        pick_b = pick.astype(f32).astype(bf16)
        tokens = pl.ds(b * BLK, BLK)
        slots = pl.ds(b * PAIR, PAIR)
        x_ref[slots, :] = mm(pick_b, n_ref[tokens, :]).astype(bf16)
        d_ref[slots, :] = mm(pick_b, dy_ref[tokens, 0:D]).astype(bf16)
        gate_ref[slots, :] = jnp.sum(jnp.where(pick, gate_row[:, b * BLK : (b + 1) * BLK], 0.0), axis=1, keepdims=True)
    x = x_ref[...]
    gate_in = mm(x, wg_ref[0])
    up_in = mm(x, wu_ref[0])
    sig = jax.nn.sigmoid(gate_in)
    silu = gate_in * sig
    inner = (silu * up_in).astype(bf16)
    out = mm(inner, wd_ref[0]).astype(bf16).astype(f32)
    gates = gate_ref[...]
    gated_ref[0] = (gates * out).astype(bf16)
    dy = d_ref[...].astype(f32)
    p = jnp.sum(dy * out, axis=-1, keepdims=True)
    high = p.astype(bf16).astype(f32)
    lane = iota((SLOTS, 128), 1)
    p_ref[0] = jnp.where(lane == HD + own, high, jnp.where(lane == HD + 32 + own, p - high, 0.0)).astype(bf16)
    slot_grad = (gates * dy).astype(bf16)
    inner_grad = mm(slot_grad, wd_ref[0], NT)
    gd_ref[0] = mm(inner, slot_grad, TN).astype(bf16)
    hg = (inner_grad * up_in * sig * (1.0 + gate_in * (1.0 - sig))).astype(bf16)
    hu = (inner_grad * silu).astype(bf16)
    hg_ref[0] = hg
    hu_ref[0] = hu
    gg_ref[0] = mm(x, hg, TN).astype(bf16)
    gu_ref[0] = mm(x, hu, TN).astype(bf16)


def return_kernel(hg_ref, hu_ref, gated_ref, p_ref, slot_ref, wg_ref, wu_ref, dx_ref, mix_ref, rows_ref):
    e = pl.program_id(0)
    rows_ref[e] = (mm(hg_ref[0], wg_ref[0], NT) + mm(hu_ref[0], wu_ref[0], NT)).astype(bf16)

    @pl.when(e == EXP_DEV - 1)
    def _():
        for b in range(PAIRS):
            tokens = pl.ds(b * BLK, BLK)
            slots = pl.ds(b * PAIR, PAIR)
            pick = jnp.concatenate(
                [pick_rows(slot_ref[k, 0:1, :], b).astype(f32).astype(bf16) for k in range(EXP_DEV)], axis=0
            )
            grads = jnp.concatenate([rows_ref[k, slots, :] for k in range(EXP_DEV)], axis=0)
            dx_ref[tokens, 0:D] = mm(pick, grads, TN).astype(bf16)
            probs = jnp.concatenate([p_ref[k, slots, :] for k in range(EXP_DEV)], axis=0)
            dx_ref[tokens, D:XW] = mm(pick, probs, TN).astype(bf16)
            outs = jnp.concatenate([gated_ref[k, slots, :] for k in range(EXP_DEV)], axis=0)
            mix_ref[tokens, :] = mm(pick, outs, TN).astype(bf16)


def hidden_kernel(part_ref, dy_ref, hidden_ref, normed_ref, gain_ref, w_ref, wo_ref, grad_ref, gain_grad_ref, send_ref):
    hidden = hidden_ref[...]
    scale = lax.rsqrt(jnp.mean(hidden * hidden, axis=-1, keepdims=True) + EPS)
    unit = hidden * scale
    total = part_ref[0].astype(f32)
    for s in range(1, OWN):
        total = total + part_ref[s].astype(f32)
    tail = total[:, D:XW]
    probs = router_probs(normed_ref[...], w_ref)
    p = tail + pltpu.roll(tail, 128 - 32, 1)
    logit_grad = probs * (p - jnp.sum(p * probs, axis=-1, keepdims=True))
    high = logit_grad.astype(bf16)
    low = (logit_grad - high.astype(f32)).astype(bf16)
    router = w_ref[:, BLK:WW]
    normed_grad = total[:, 0:D] + mm(high, router, NT) + mm(low, router, NT)
    gain_grad_ref[...] = jnp.sum(normed_grad * unit, axis=0, keepdims=True)
    unit_grad = normed_grad * gain_ref[...]
    grad = dy_ref[...].astype(f32) + scale * (unit_grad - unit * jnp.mean(unit_grad * unit, axis=-1, keepdims=True))
    grad_ref[...] = grad
    branch = grad.astype(bf16)
    for j in range(OWN):
        cols = slice(j * QW, (j + 1) * QW)
        send_ref[j, :, 0:QW] = mm(branch, wo_ref[cols, :], NT).astype(bf16)
        send_ref[j, :, QW : 2 * QW] = grad[:, cols].astype(bf16)
        send_ref[j, :, 2 * QW : 2 * QW + 128] = high


def attend_back_kernel(qkv_ref, log_ref, g_ref, cos_ref, sin_ref, start_ref, dqkv_ref, turn_ref, dk_ref, dv_ref):
    dk_ref[...] = jnp.zeros_like(dk_ref)
    dv_ref[...] = jnp.zeros_like(dv_ref)
    for at in range(0, GROUP, BLK):
        rows = pl.ds(at, BLK)
        keys = at + BLK
        seen = block_mask(start_ref, at, keys)
        k_h = qkv_ref[0:keys, QW : QW + HD]
        v_h = qkv_ref[0:keys, BLK : BLK + HD]
        for r in range(HEADS):
            q_h = qkv_ref[rows, r * HD : (r + 1) * HD] * jnp.asarray(HD**-0.5, bf16)
            g_h = g_ref[rows, r * HD : (r + 1) * HD]
            scores = jnp.where(seen, mm(q_h, k_h, NT), -1e30)
            prob = jnp.exp(scores - log_ref[rows, r : r + 1])
            dv_ref[0:keys, :] += mm(prob.astype(bf16), g_h, TN)
            prob_grad = mm(g_h, v_h, NT)
            delta = jnp.sum(prob_grad * prob, axis=-1, keepdims=True)
            score_grad = (prob * (prob_grad - delta)).astype(bf16)
            turn_ref[rows, r * HD : (r + 1) * HD] = mm(score_grad, k_h) * (HD**-0.5)
            dk_ref[0:keys, :] += mm(score_grad, q_h, TN)
    turn_ref[:, QW : QW + HD] = dk_ref[...]
    for at in range(0, GROUP, BLK):
        rows = pl.ds(at, BLK)
        turned = turn_ref[rows, :]
        turned = turned * cos_ref[rows, :] - swap_halves(turned) * sin_ref[rows, :]
        dqkv_ref[rows, 0:BLK] = turned.astype(bf16)
        dqkv_ref[rows, BLK : BLK + HD] = dv_ref[rows, :].astype(bf16)
        dqkv_ref[rows, BLK + HD : WW] = jnp.zeros((BLK, WW - BLK - HD), bf16)


def weight_kernel(normed_ref, dqkv_ref, mix_ref, got_ref, n_ref, moe_gain_ref, x_ref, w_ref, back_ref, pay_ref, gain_ref):
    gain_ref[...] = jnp.zeros_like(gain_ref)
    for at in range(0, GROUP, BLK):
        rows = pl.ds(at, BLK)
        back = mm(dqkv_ref[rows, :], w_ref[...], NT)
        back_ref[rows, :] = back.astype(bf16)
        x = x_ref[rows, :].astype(f32)
        unit = x * lax.rsqrt(jnp.mean(x * x, axis=-1, keepdims=True) + EPS)
        gain_ref[0:1, :] += jnp.sum(back * unit, axis=0, keepdims=True)
    pay_ref[:, 0:BLK] = mm(normed_ref[...], dqkv_ref[:, 0:BLK], TN).astype(bf16)
    hid = got_ref[:, 128:WW]
    hid = jnp.where(iota((GROUP, BLK), 1) < HD, jnp.zeros_like(hid), hid)
    value = jnp.concatenate([dqkv_ref[:, BLK:WW], jnp.zeros((GROUP, 128), bf16)], axis=1)
    pay_ref[:, BLK : 2 * BLK] = (mm(normed_ref[...], value, TN) + mm(mix_ref[...], hid, TN)).astype(bf16)
    router = mm(n_ref[...], got_ref[:, 2 * QW : 2 * QW + 128], TN)
    attn_gain = jnp.transpose(jnp.broadcast_to(gain_ref[0:1, :], (128, D)))
    moe_gain = jnp.transpose(jnp.broadcast_to(moe_gain_ref[...], (128, D)))
    lane = iota((D, 128), 1)
    tail = jnp.where(lane == 0, attn_gain, jnp.where(lane == 1, moe_gain, jnp.where(lane >= HD, router, 0.0)))
    pay_ref[:, 2 * BLK : 2 * BLK + 128] = tail.astype(bf16)


def input_kernel(part_ref, x_ref, gain_ref, hidden_grad_ref, out_ref):
    x = x_ref[...].astype(f32)
    scale = lax.rsqrt(jnp.mean(x * x, axis=-1, keepdims=True) + EPS)
    unit = x * scale
    total = part_ref[0].astype(f32)
    for s in range(1, OWN):
        total = total + part_ref[s].astype(f32)
    unit_grad = total * gain_ref[...]
    out_ref[...] = (
        hidden_grad_ref[...] + scale * (unit_grad - unit * jnp.mean(unit_grad * unit, axis=-1, keepdims=True))
    ).astype(bf16)


def sds(shape, dtype):
    return jax.ShapeDtypeStruct(shape, dtype)


def call(kernel, outs, scratch=(), cost=None, **grid):
    return pl.pallas_call(
        kernel,
        out_shape=outs,
        scratch_shapes=list(scratch),
        compiler_params=pltpu.CompilerParams(vmem_limit_bytes=VMEM),
        cost_estimate=cost,
        **grid,
    )


def cost(gmac, mbytes):
    return pl.CostEstimate(flops=int(2e9 * gmac), bytes_accessed=int(1e6 * mbytes), transcendentals=0)


def body(
    tokens, norm_attn, query_weight, key_weight, value_weight, out_weight, norm_moe, router_weight,
    gate_weight, up_weight, down_weight, routes, seq_lengths, out_grad,
):
    own = lax.axis_index("expert")
    gain_one = norm_attn.reshape(1, D)
    gain_two = norm_moe.reshape(1, D)

    shard = jnp.concatenate(
        [
            lax.dynamic_slice_in_dim(query_weight, own * QW, QW, 1),
            lax.dynamic_slice_in_dim(key_weight, own * HD, HD, 1),
            lax.dynamic_slice_in_dim(value_weight, own * HD, HD, 1),
            router_weight,
            jnp.zeros((D // DP, WW - BLK - HD - EXPERTS), bf16),
        ],
        axis=1,
    )
    weights = lax.all_to_all(
        jnp.broadcast_to(shard[None], (DP, D // DP, WW)), "dp", 0, 0, tiled=True
    ).reshape(D, WW)
    x_all = lax.all_gather(tokens, "expert", axis=0, tiled=True)
    out_full = lax.all_gather(out_weight, "dp", axis=0, tiled=True)
    dy_own = jnp.concatenate([out_grad, routes.astype(bf16), jnp.zeros((ROWS, XW - D - TOP), bf16)], axis=1)
    dy_all = lax.all_gather(dy_own, "expert", axis=0, tiled=True)
    routes_t = dy_all[:, D : D + TOP].T.astype(jnp.int32)

    end_one = seq_lengths[0, 0]
    end_two = end_one + seq_lengths[0, 1]
    place = jnp.arange(GROUP, dtype=jnp.int32)
    start = jnp.where(place >= end_two, end_two, jnp.where(place >= end_one, end_one, 0)).astype(jnp.int32)
    steps = jnp.arange(HD // 2, dtype=f32)
    freq = jnp.exp(steps * (-2.0 * math.log(THETA) / HD))
    angles = (place - start).astype(f32)[:, None] * freq[None, :]
    cos_half, sin_half = jnp.cos(angles), jnp.sin(angles)
    cos_t = jnp.tile(cos_half, (1, 8))
    sin_t = jnp.tile(jnp.concatenate([-sin_half, sin_half], axis=1), (1, 4))
    start = start.reshape(GROUP, 1)

    normed_one, qkv, mix, logs = call(
        attend_kernel,
        [sds((GROUP, D), bf16), sds((GROUP, WW), bf16), sds((GROUP, QW), bf16), sds((GROUP, 8), f32)],
        cost=cost(2, 10),
    )(x_all, weights, gain_one, cos_t, sin_t, start)

    mix_own = lax.all_to_all(mix, "expert", 0, 0, tiled=True).reshape(OWN, ROWS, QW)
    hidden, normed_two = call(out_kernel, [sds((ROWS, D), f32), sds((ROWS, D), bf16)], cost=cost(0.5, 6))(
        mix_own, out_full, tokens, gain_two
    )
    n_all = lax.all_gather(normed_two, "expert", axis=0, tiled=True)

    whole = lambda *shape: pl.BlockSpec(shape, lambda e: (0,) * len(shape), pipeline_mode=pl.Buffered(1))
    each = lambda *shape: pl.BlockSpec((1,) + shape, lambda e: (e, 0, 0))
    gg, gu, gd, hg, hu, gated, p_slots, slot_rows = call(
        expert_kernel,
        [
            sds((EXP_DEV, D, FFE), bf16), sds((EXP_DEV, D, FFE), bf16), sds((EXP_DEV, FFE, D), bf16),
            sds((EXP_DEV, SLOTS, FFE), bf16), sds((EXP_DEV, SLOTS, FFE), bf16), sds((EXP_DEV, SLOTS, D), bf16),
            sds((EXP_DEV, SLOTS, 128), bf16), sds((EXP_DEV, 8, GROUP), jnp.int32),
        ],
        scratch=[
            pltpu.VMEM((128, GROUP), f32), pltpu.VMEM((SLOTS, D), bf16), pltpu.VMEM((SLOTS, D), bf16),
            pltpu.VMEM((SLOTS, 1), f32),
        ],
        cost=cost(9, 45),
        grid=(EXP_DEV,),
        in_specs=[
            pl.BlockSpec(memory_space=pltpu.SMEM), whole(GROUP, D), whole(GROUP, XW), whole(TOP, GROUP), whole(D, WW),
            each(D, FFE), each(D, FFE), each(FFE, D),
        ],
        out_specs=[
            each(D, FFE), each(D, FFE), each(FFE, D), each(SLOTS, FFE), each(SLOTS, FFE), each(SLOTS, D),
            each(SLOTS, 128), each(8, GROUP),
        ],
    )(own.reshape(1).astype(jnp.int32), n_all, dy_all, routes_t, weights, gate_weight, up_weight, down_weight)

    down_total, gate_total, up_total = lax.psum((gd, gg, gu), "dp")

    dx_part, mix_part = call(
        return_kernel,
        [sds((GROUP, XW), bf16), sds((GROUP, D), bf16)],
        scratch=[pltpu.VMEM((EXP_DEV, SLOTS, D), bf16)],
        cost=cost(4, 20),
        grid=(EXP_DEV,),
        in_specs=[
            each(SLOTS, FFE), each(SLOTS, FFE), whole(EXP_DEV, SLOTS, D), whole(EXP_DEV, SLOTS, 128),
            whole(EXP_DEV, 8, GROUP), each(D, FFE), each(D, FFE),
        ],
        out_specs=[whole(GROUP, XW), whole(GROUP, D)],
    )(hg, hu, gated, p_slots, slot_rows, gate_weight, up_weight)

    dx_parts = lax.all_to_all(dx_part, "expert", 0, 0, tiled=True).reshape(OWN, ROWS, XW)
    hidden_grad, moe_gain, send = call(
        hidden_kernel,
        [sds((ROWS, D), f32), sds((1, D), f32), sds((OWN, ROWS, 512), bf16)],
        cost=cost(0.6, 10),
    )(dx_parts, out_grad, hidden, normed_two, gain_two, weights, out_full)
    got = lax.all_to_all(send.reshape(GROUP, 512), "expert", 0, 0, tiled=True)
    dqkv = call(
        attend_back_kernel,
        sds((GROUP, WW), bf16),
        scratch=[pltpu.VMEM((GROUP, BLK), f32), pltpu.VMEM((GROUP, HD), f32), pltpu.VMEM((GROUP, HD), f32)],
        cost=cost(4, 8),
    )(qkv, logs, got, cos_t, sin_t, start)
    mix_all = lax.all_to_all(
        jnp.broadcast_to(jnp.moveaxis(mix_own, 0, 1).reshape(1, ROWS, D), (OWN, ROWS, D)).reshape(GROUP, D),
        "expert", 0, 0, tiled=True,
    )
    back_part, pay = call(
        weight_kernel,
        [sds((GROUP, D), bf16), sds((D, 640), bf16)],
        scratch=[pltpu.VMEM((8, D), f32)],
        cost=cost(2, 20),
    )(normed_one, dqkv, mix_all, got, n_all, moe_gain, x_all, weights)

    pay_parts = lax.all_to_all(pay, "dp", 0, 0, tiled=True).reshape(DP, D // DP, 640)
    back_parts = lax.all_to_all(back_part, "expert", 0, 0, tiled=True).reshape(OWN, ROWS, D)
    pay_own = jnp.sum(pay_parts.astype(f32), axis=0)
    pay_all = lax.all_to_all(
        jnp.broadcast_to(pay_own.astype(bf16)[None], (OWN, D // DP, 640)), "expert", 0, 0, tiled=True
    )
    join = lambda lo, hi: jnp.moveaxis(pay_all[:, :, lo:hi], 0, 1).reshape(D // DP, OWN * (hi - lo)).astype(f32)
    query_total, key_total, value_total, out_total = join(0, QW), join(QW, BLK), join(BLK, BLK + HD), join(BLK + HD, 512)
    router_total = pay_own[:, 512 + HD : 512 + HD + EXPERTS]
    gains = jnp.sum(pay_all[:, :, 512:514].astype(f32), axis=0).T.reshape(1, 2, D // DP)
    gains = jnp.pad(gains, ((0, 0), (0, 6), (0, 32)))
    gains = lax.all_to_all(jnp.broadcast_to(gains, (DP, 8, 128)), "dp", 0, 0, tiled=True)
    gain_attn = gains[:, 0, : D // DP].reshape(D)
    gain_moe = gains[:, 1, : D // DP].reshape(D)

    input_grad = call(input_kernel, sds((ROWS, D), bf16), cost=cost(0, 6))(back_parts, tokens, gain_one, hidden_grad)
    mix_parts = lax.all_to_all(mix_part, "expert", 0, 0, tiled=True).reshape(OWN, ROWS, D)
    layer_out = (hidden + jnp.sum(mix_parts.astype(f32), axis=0)).astype(bf16)
    return (
        layer_out, input_grad, gain_attn, query_total, key_total, value_total, out_total, gain_moe, router_total,
        gate_total.astype(f32), up_total.astype(f32), down_total.astype(f32),
    )


def solution(mesh):
    both, dp, expert = P(("dp", "expert"), None), P("dp", None), P("expert", None, None)
    return jax.shard_map(
        body,
        mesh=mesh,
        in_specs=(both, P(), dp, dp, dp, dp, P(), dp, expert, expert, expert, both, dp, both),
        out_specs=(both, both, P(), dp, dp, dp, dp, P(), dp, expert, expert, expert),
        check_vma=False,
    )
```

```python
import functools
import math

import jax
import jax.numpy as jnp
from jax import lax
from jax.experimental import pallas as pl
from jax.experimental.pallas import tpu as pltpu
from jax.sharding import PartitionSpec as P

QH = 24
KVH = 8
HD = 64
TOP = 8
EXP_DEV = 3
CAP = 56
D = 1536
FFE = 512
ROWS = 128
OWN = 8
GROUP = 1024
DP = 16
EXPERTS = 24
HEADS = 3
QW = HEADS * HD
PAIR = 2 * CAP
PAIRS = OWN // 2
SLOTS = OWN * CAP
BLK = 256
WW = 384
XW = D + 128
PW = 2 * D + 128
HALF = D // 2
EPS = 1e-06
THETA = 10000.0
VMEM = 60 * 1024 * 1024
f32 = jnp.float32
bf16 = jnp.bfloat16

NN = (((1,), (0,)), ((), ()))
NT = (((1,), (1,)), ((), ()))
TN = (((0,), (0,)), ((), ()))


def mm(a, b, dims=NN):
    return lax.dot_general(a, b, dims, preferred_element_type=f32)


def iota(shape, dim):
    return lax.broadcasted_iota(jnp.int32, shape, dim)


def swap_halves(v):
    lane = iota(v.shape, 1) % HD
    width = v.shape[1]
    ahead = pltpu.roll(v, width - HD // 2, 1)
    behind = pltpu.roll(v, HD // 2, 1)
    return jnp.where(lane < HD // 2, ahead, behind)


def block_mask(start_ref, at, keys):
    place = at + iota((BLK, keys), 0)
    key = iota((BLK, keys), 1)
    first = start_ref[pl.ds(at, BLK), :]
    return (key <= place) & (key >= first)


def prep_kernel(
    own_ref, wq_ref, wk_ref, wv_ref, wr_ref, wo_ref, x_ref, dy_ref, routes_ref, shard_ref, half_ref, rows_ref, own_cols
):
    own = own_ref[0]
    rows_ref[:, 0:D] = x_ref[...]
    rows_ref[:, D : 2 * D] = dy_ref[...]
    rows_ref[:, 2 * D : PW] = jnp.zeros((ROWS, PW - 2 * D), bf16)
    rows_ref[:, 2 * D : 2 * D + TOP] = routes_ref[...].astype(f32).astype(bf16)
    own_cols[...] = jnp.zeros_like(own_cols)
    for j in range(OWN):

        @pl.when(own == j)
        def _(j=j):
            own_cols[:, 0:QW] = wq_ref[:, j * QW : (j + 1) * QW]
            own_cols[:, QW:BLK] = wk_ref[:, j * HD : (j + 1) * HD]
            own_cols[:, BLK : BLK + HD] = wv_ref[:, j * HD : (j + 1) * HD]

    own_cols[:, BLK + HD : BLK + HD + EXPERTS] = wr_ref[...]
    shard_ref[...] = jnp.broadcast_to(own_cols[...][None], shard_ref.shape)
    half_ref[...] = jnp.where(own % 2 == 0, wo_ref[:, 0:HALF], wo_ref[:, HALF:D])


def gate_kernel(in_ref, after_ref, out_ref):
    pass


def owner_of(own, dz, dc):
    return ((own // 2 + dz) % 4) * 2 + (own + dc) % 2


def pieces_of(refs):
    near, up, down, far_a, far_b = range(5)
    for dc in range(2):
        mine = refs[dc * 5 : dc * 5 + 5]
        yield 0, dc, lambda mine=mine: mine[near][...]
        yield 1, dc, lambda mine=mine: mine[down][...]
        yield 3, dc, lambda mine=mine: mine[up][...]
        yield 2, dc, lambda mine=mine: jnp.concatenate([mine[far_a][...], mine[far_b][...]], axis=0)


def attend_kernel(own_ref, *refs):
    x_refs, refs = refs[:10], refs[10:]
    w_ref, gain_ref, cos_ref, sin_ref, start_ref, normed_ref, qkv_ref, mix_ref, log_ref = refs
    own = own_ref[0]
    for dz, dc, load in pieces_of(x_refs):
        rows = pl.ds(pl.multiple_of(owner_of(own, dz, dc) * ROWS, ROWS), ROWS)
        x = load().astype(f32)
        scale = lax.rsqrt(jnp.mean(x * x, axis=-1, keepdims=True) + EPS)
        normed = (x * scale * gain_ref[...]).astype(bf16)
        normed_ref[rows, :] = normed
        raw = mm(normed, w_ref[...])
        turned = raw[:, :BLK]
        turned = turned * cos_ref[rows, :] + swap_halves(turned) * sin_ref[rows, :]
        qkv_ref[rows, 0:BLK] = turned.astype(bf16)
        qkv_ref[rows, BLK:WW] = raw[:, BLK:WW].astype(bf16)
    for at in range(0, GROUP, BLK):
        rows = pl.ds(at, BLK)
        keys = at + BLK
        seen = block_mask(start_ref, at, keys)
        k_h = qkv_ref[0:keys, QW : QW + HD]
        v_h = qkv_ref[0:keys, BLK : BLK + HD]
        outs = []
        for r in range(HEADS):
            q_h = qkv_ref[rows, r * HD : (r + 1) * HD] * jnp.asarray(HD**-0.5, bf16)
            scores = jnp.where(seen, mm(q_h, k_h, NT), -1e30)
            top = jnp.max(scores, axis=-1, keepdims=True)
            terms = jnp.exp(scores - top)
            total = jnp.sum(terms, axis=-1, keepdims=True)
            prob = (terms / total).astype(bf16)
            outs.append(mm(prob, v_h))
            log_ref[rows, r : r + 1] = top + jnp.log(total)
        block = jnp.concatenate(outs + [jnp.zeros_like(outs[0])], axis=1).astype(bf16)
        mix_ref[at // ROWS] = block[0:ROWS]
        mix_ref[at // ROWS + 1] = block[ROWS:BLK]


def out_kernel(own_ref, mix_ref, mine_ref, other_ref, x_ref, gain_ref, hidden_ref, normed_ref, flat_ref):
    core = own_ref[0] % 2
    for j in range(OWN):
        flat_ref[:, j * QW : (j + 1) * QW] = mix_ref[j, :, 0:QW]
    flat = flat_ref[...]
    for at, wo_ref in ((core, mine_ref), (1 - core, other_ref)):
        cols = pl.ds(pl.multiple_of(at * HALF, 128), HALF)
        hidden_ref[:, cols] = x_ref[:, cols].astype(f32) + mm(flat, wo_ref[...])
    hidden = hidden_ref[...]
    scale = lax.rsqrt(jnp.mean(hidden * hidden, axis=-1, keepdims=True) + EPS)
    normed_ref[...] = (hidden * scale * gain_ref[...]).astype(bf16)


def router_probs(normed, w_ref):
    logits = mm(normed, w_ref[:, BLK:WW])
    lane = iota(logits.shape, 1)
    real = (lane >= HD) & (lane < HD + EXPERTS)
    logits = jnp.where(real, logits, -1e30)
    terms = jnp.exp(logits - jnp.max(logits, axis=-1, keepdims=True))
    terms = jnp.where(real, terms, 0.0)
    return terms / jnp.sum(terms, axis=-1, keepdims=True)


def pick_rows(slot_row, b):
    row = slot_row[:, b * BLK : (b + 1) * BLK]
    return iota((PAIR, BLK), 0) == row


def expert_kernel(own_ref, *refs):
    dy_refs, route_refs, refs = refs[:10], refs[10:20], refs[20:]
    n_ref, w_ref, wg_ref, wu_ref, wd_ref, gg_ref, gu_ref, gd_ref, hg_ref, hu_ref = refs[:10]
    gated_ref, p_ref, slot_ref, prob_ref, x_ref, d_ref, gate_ref, dy_ref, routes_ref = refs[10:]
    e = pl.program_id(0)
    own = own_ref[0] * EXP_DEV + e

    @pl.when(e == 0)
    def _():
        for at in range(0, GROUP, BLK):
            probs = router_probs(n_ref[at : at + BLK, :], w_ref)
            prob_ref[:, at : at + BLK] = jnp.transpose(probs)
        for dz, dc, load in pieces_of(dy_refs):
            rows = pl.ds(pl.multiple_of(owner_of(own_ref[0], dz, dc) * ROWS, ROWS), ROWS)
            dy_ref[rows, :] = load()
        for dz, dc, load in pieces_of(route_refs):
            rows = pl.ds(pl.multiple_of(owner_of(own_ref[0], dz, dc) * ROWS, ROWS), ROWS)
            routes_ref[:, rows] = jnp.transpose(load().astype(f32))[0:TOP]

    chosen = jnp.max((routes_ref[...] == own.astype(f32)).astype(f32), axis=0, keepdims=True)
    gate_row = jnp.sum(jnp.where(iota((128, GROUP), 0) == HD + own, prob_ref[...], 0.0), axis=0, keepdims=True)
    before = (iota((ROWS, ROWS), 0) < iota((ROWS, ROWS), 1)).astype(f32).astype(bf16)
    ranks = []
    for s in range(OWN):
        part = jnp.broadcast_to(chosen[:, s * ROWS : (s + 1) * ROWS], (8, ROWS)).astype(bf16)
        ranks.append(mm(part, before)[0:1] + float(CAP * (s % 2)))
    rank = jnp.concatenate(ranks, axis=1)
    slot_row = jnp.where(chosen > 0.0, rank, -1.0).astype(jnp.int32)
    slot_ref[0] = jnp.broadcast_to(slot_row, (8, GROUP))
    for b in range(PAIRS):
        pick = pick_rows(slot_row, b)
        pick_b = pick.astype(f32).astype(bf16)
        tokens = pl.ds(b * BLK, BLK)
        slots = pl.ds(b * PAIR, PAIR)
        x_ref[slots, :] = mm(pick_b, n_ref[tokens, :]).astype(bf16)
        d_ref[slots, :] = mm(pick_b, dy_ref[tokens, :]).astype(bf16)
        gate_ref[slots, :] = jnp.sum(jnp.where(pick, gate_row[:, b * BLK : (b + 1) * BLK], 0.0), axis=1, keepdims=True)
    x = x_ref[...]
    gate_in = mm(x, wg_ref[0])
    up_in = mm(x, wu_ref[0])
    sig = jax.nn.sigmoid(gate_in)
    silu = gate_in * sig
    inner = (silu * up_in).astype(bf16)
    out = mm(inner, wd_ref[0]).astype(bf16).astype(f32)
    gates = gate_ref[...]
    gated_ref[0] = (gates * out).astype(bf16)
    dy = d_ref[...].astype(f32)
    p = jnp.sum(dy * out, axis=-1, keepdims=True)
    high = p.astype(bf16).astype(f32)
    lane = iota((SLOTS, 128), 1)
    p_ref[0] = jnp.where(lane == HD + own, high, jnp.where(lane == HD + 32 + own, p - high, 0.0)).astype(bf16)
    slot_grad = (gates * dy).astype(bf16)
    inner_grad = mm(slot_grad, wd_ref[0], NT)
    gd_ref[0] = mm(inner, slot_grad, TN).astype(bf16)
    hg = (inner_grad * up_in * sig * (1.0 + gate_in * (1.0 - sig))).astype(bf16)
    hu = (inner_grad * silu).astype(bf16)
    hg_ref[0] = hg
    hu_ref[0] = hu
    gg_ref[0] = mm(x, hg, TN).astype(bf16)
    gu_ref[0] = mm(x, hu, TN).astype(bf16)


def split_core(core, both):
    first, second = both[0:ROWS], both[ROWS:BLK]
    return jnp.where(core == 0, first, second), jnp.where(core == 0, second, first)


def scatter_pairs(own, slot_ref, parts):
    for dz in range(PAIRS):
        b = (own // 2 + dz) % PAIRS
        tokens = pl.ds(pl.multiple_of(b * BLK, BLK), BLK)
        slots = pl.ds(pl.multiple_of(b * PAIR, PAIR), PAIR)
        pick = jnp.concatenate(
            [(iota((PAIR, BLK), 0) == slot_ref[k, 0:1, tokens]).astype(f32).astype(bf16) for k in range(EXP_DEV)],
            axis=0,
        )
        for ref, width, at, keep_ref, send_ref in parts:
            values = jnp.concatenate([ref[k, slots, :] for k in range(EXP_DEV)], axis=0)
            keep, send = split_core(own % 2, mm(pick, values, TN))
            keep_ref[dz, :, at : at + width] = keep.astype(bf16)
            send_ref[dz, :, at : at + width] = send.astype(bf16)


def return_kernel(own_ref, hg_ref, hu_ref, p_ref, slot_ref, wg_ref, wu_ref, keep_ref, send_ref, rows_ref):
    e = pl.program_id(0)
    rows_ref[e] = (mm(hg_ref[0], wg_ref[0], NT) + mm(hu_ref[0], wu_ref[0], NT)).astype(bf16)

    @pl.when(e == EXP_DEV - 1)
    def _():
        scatter_pairs(
            own_ref[0], slot_ref, ((rows_ref, D, 0, keep_ref, send_ref), (p_ref, 128, D, keep_ref, send_ref))
        )


def mixture_kernel(own_ref, gated_ref, slot_ref, keep_ref, send_ref):
    scatter_pairs(own_ref[0], slot_ref, ((gated_ref, D, 0, keep_ref, send_ref),))


def hidden_kernel(
    own_ref, part_a, part_b, part_c, dy_ref, hidden_ref, normed_ref, gain_ref, w_ref, mine_ref, other_ref,
    grad_ref, gain_grad_ref, send_ref, cols_ref,
):
    core = own_ref[0] % 2
    hidden = hidden_ref[...]
    scale = lax.rsqrt(jnp.mean(hidden * hidden, axis=-1, keepdims=True) + EPS)
    unit = hidden * scale
    total = part_a[0].astype(f32) + part_b[...].astype(f32) + part_c[...].astype(f32)
    tail = total[:, D:XW]
    probs = router_probs(normed_ref[...], w_ref)
    p = tail + pltpu.roll(tail, 128 - 32, 1)
    logit_grad = probs * (p - jnp.sum(p * probs, axis=-1, keepdims=True))
    high = logit_grad.astype(bf16)
    low = (logit_grad - high.astype(f32)).astype(bf16)
    router = w_ref[:, BLK:WW]
    normed_grad = total[:, 0:D] + mm(high, router, NT) + mm(low, router, NT)
    gain_grad_ref[...] = jnp.sum(normed_grad * unit, axis=0, keepdims=True)
    unit_grad = normed_grad * gain_ref[...]
    grad = dy_ref[...].astype(f32) + scale * (unit_grad - unit * jnp.mean(unit_grad * unit, axis=-1, keepdims=True))
    grad_ref[...] = grad
    mix_grad = jnp.zeros((ROWS, D), f32)
    for at, wo_ref in ((core, mine_ref), (1 - core, other_ref)):
        cols = pl.ds(pl.multiple_of(at * HALF, 128), HALF)
        mix_grad = mix_grad + mm(grad_ref[:, cols].astype(bf16), wo_ref[...], NT)
    for j in range(OWN):
        cols = slice(j * QW, (j + 1) * QW)
        send_ref[j, :, 0:QW] = mix_grad[:, cols].astype(bf16)
        send_ref[j, :, QW:BLK] = jnp.zeros((ROWS, BLK - QW), bf16)
        cols_ref[j, :, 0:HD] = jnp.zeros((ROWS, HD), bf16)
        cols_ref[j, :, HD:BLK] = grad[:, cols].astype(bf16)
        cols_ref[j, :, BLK:WW] = high


def attend_back_kernel(qkv_ref, log_ref, g_ref, cos_ref, sin_ref, start_ref, dqkv_ref, turn_ref, dk_ref, dv_ref):
    dk_ref[...] = jnp.zeros_like(dk_ref)
    dv_ref[...] = jnp.zeros_like(dv_ref)
    for at in range(0, GROUP, BLK):
        rows = pl.ds(at, BLK)
        keys = at + BLK
        seen = block_mask(start_ref, at, keys)
        k_h = qkv_ref[0:keys, QW : QW + HD]
        v_h = qkv_ref[0:keys, BLK : BLK + HD]
        for r in range(HEADS):
            q_h = qkv_ref[rows, r * HD : (r + 1) * HD] * jnp.asarray(HD**-0.5, bf16)
            g_h = g_ref[rows, r * HD : (r + 1) * HD]
            scores = jnp.where(seen, mm(q_h, k_h, NT), -1e30)
            prob = jnp.exp(scores - log_ref[rows, r : r + 1])
            dv_ref[0:keys, :] += mm(prob.astype(bf16), g_h, TN)
            prob_grad = mm(g_h, v_h, NT)
            delta = jnp.sum(prob_grad * prob, axis=-1, keepdims=True)
            score_grad = (prob * (prob_grad - delta)).astype(bf16)
            turn_ref[rows, r * HD : (r + 1) * HD] = mm(score_grad, k_h) * (HD**-0.5)
            dk_ref[0:keys, :] += mm(score_grad, q_h, TN)
    turn_ref[:, QW : QW + HD] = dk_ref[...]
    for at in range(0, GROUP, BLK):
        rows = pl.ds(at, BLK)
        turned = turn_ref[rows, :]
        turned = turned * cos_ref[rows, :] - swap_halves(turned) * sin_ref[rows, :]
        dqkv_ref[rows, 0:BLK] = turned.astype(bf16)
        dqkv_ref[rows, BLK : BLK + HD] = dv_ref[rows, :].astype(bf16)
        dqkv_ref[rows, BLK + HD : WW] = jnp.zeros((BLK, WW - BLK - HD), bf16)


def weight_kernel(
    own_ref, normed_ref, dqkv_ref, mix_ref, got_ref, n_ref, moe_gain_ref, norm_ref, w_ref,
    keep_ref, send_ref, pay_ref, gain_ref,
):
    own = own_ref[0]
    gain_ref[...] = jnp.zeros_like(gain_ref)
    for dz in range(PAIRS):
        b = (own // 2 + dz) % PAIRS
        rows = pl.ds(pl.multiple_of(b * BLK, BLK), BLK)
        back = mm(dqkv_ref[rows, :], w_ref[...], NT)
        gain_ref[0:1, :] += jnp.sum(back * normed_ref[rows, :].astype(f32), axis=0, keepdims=True)
        keep, send = split_core(own % 2, back)
        keep_ref[dz] = keep.astype(bf16)
        send_ref[dz] = send.astype(bf16)
    pay_ref[:, 0:BLK] = mm(normed_ref[...], dqkv_ref[:, 0:BLK], TN).astype(bf16)
    value = jnp.concatenate([dqkv_ref[:, BLK:WW], jnp.zeros((GROUP, 128), bf16)], axis=1)
    pay_ref[:, BLK : 2 * BLK] = (mm(normed_ref[...], value, TN) + mm(mix_ref[...], got_ref[:, 0:BLK], TN)).astype(bf16)
    router = mm(n_ref[...], got_ref[:, BLK:WW], TN)
    attn_gain = jnp.transpose(jnp.broadcast_to(gain_ref[0:1, :] / norm_ref[...], (128, D)))
    moe_gain = jnp.transpose(jnp.broadcast_to(moe_gain_ref[...], (128, D)))
    lane = iota((D, 128), 1)
    tail = jnp.where(lane == 0, attn_gain, jnp.where(lane == 1, moe_gain, jnp.where(lane >= HD, router, 0.0)))
    pay_ref[:, 2 * BLK : 2 * BLK + 128] = tail.astype(bf16)


def input_kernel(part_a, part_b, part_c, x_ref, gain_ref, hidden_grad_ref, out_ref):
    x = x_ref[...].astype(f32)
    scale = lax.rsqrt(jnp.mean(x * x, axis=-1, keepdims=True) + EPS)
    unit = x * scale
    total = part_a[0].astype(f32) + part_b[...].astype(f32) + part_c[...].astype(f32)
    unit_grad = total * gain_ref[...]
    out_ref[...] = (
        hidden_grad_ref[...] + scale * (unit_grad - unit * jnp.mean(unit_grad * unit, axis=-1, keepdims=True))
    ).astype(bf16)


def layer_kernel(part_a, part_b, part_c, hidden_ref, out_ref):
    total = part_a[0].astype(f32) + part_b[...].astype(f32) + part_c[...].astype(f32)
    out_ref[...] = (hidden_ref[...] + total).astype(bf16)


def sum_kernel(part_ref, sum_ref, router_ref):
    total = part_ref[0].astype(f32)
    for s in range(1, DP):
        total = total + part_ref[s].astype(f32)
    sum_ref[...] = jnp.broadcast_to(total.astype(bf16)[None], sum_ref.shape)
    router_ref[...] = total[:, 2 * BLK + HD : 2 * BLK + HD + EXPERTS]


def join_kernel(part_ref, q_ref, k_ref, v_ref, o_ref, gain_ref):
    gains = jnp.zeros((D // DP, 128), f32)
    for j in range(OWN):
        part = part_ref[j].astype(f32)
        q_ref[:, j * QW : (j + 1) * QW] = part[:, 0:QW]
        k_ref[:, j * HD : (j + 1) * HD] = part[:, QW:BLK]
        v_ref[:, j * HD : (j + 1) * HD] = part[:, BLK : BLK + HD]
        o_ref[:, j * QW : (j + 1) * QW] = part[:, BLK + HD : 2 * BLK]
        gains = gains + part[:, 2 * BLK : 2 * BLK + 128]
    gains = jnp.concatenate([gains, jnp.zeros((128 - D // DP, 128), f32)], axis=0)
    gain_ref[...] = jnp.broadcast_to(jnp.transpose(gains)[0:8][None], gain_ref.shape)


def sds(shape, dtype):
    return jax.ShapeDtypeStruct(shape, dtype)


def call(kernel, outs, scratch=(), cost=None, **grid):
    return pl.pallas_call(
        kernel,
        out_shape=outs,
        scratch_shapes=list(scratch),
        compiler_params=pltpu.CompilerParams(vmem_limit_bytes=VMEM),
        cost_estimate=cost,
        **grid,
    )


def cost(micros):
    return pl.CostEstimate(flops=int(micros * 1.15e9), bytes_accessed=1024, transcendentals=0)


VM = pl.BlockSpec(memory_space=pltpu.VMEM)
SM = pl.BlockSpec(memory_space=pltpu.SMEM)
ANY = pl.BlockSpec(memory_space=pl.ANY)


def along_z(step):
    return [(i, ((i // 2 + step) % 4) * 2 + i % 2) for i in range(OWN)]


UP, DOWN, SWAP = along_z(1), along_z(-1), [(i, i ^ 1) for i in range(OWN)]


def move(value, pairs):
    return lax.ppermute(value, "expert", pairs)


def gate(value, after):
    return pl.pallas_call(
        gate_kernel,
        out_shape=sds(value.shape, value.dtype),
        in_specs=[ANY, ANY],
        out_specs=ANY,
        input_output_aliases={0: 0},
        compiler_params=pltpu.CompilerParams(vmem_limit_bytes=VMEM),
        cost_estimate=cost(0.5),
    )(value, after)


def gather_rows(value):
    half = value.shape[0] // 2
    up, down = move(value, UP), move(value, DOWN)
    far_a, far_b = move(up[:half], UP), move(down[half:], DOWN)
    mine = [value, up, down, far_a, far_b]
    return mine + [move(piece, SWAP) for piece in mine]


def add(left, right):
    return (left.astype(f32) + right.astype(f32)).astype(bf16)


def scatter_rows(keep, send):
    half = ROWS // 2
    both = add(keep, move(send, SWAP))
    up, down = move(both[2, :half], UP), move(both[2, half:], DOWN)
    first = jnp.concatenate([add(both[1, :half], up), both[1, half:]], axis=0)
    last = jnp.concatenate([both[3, :half], add(both[3, half:], down)], axis=0)
    return both, move(first, UP), move(last, DOWN)


def body(
    tokens, norm_attn, query_weight, key_weight, value_weight, out_weight, norm_moe, router_weight,
    gate_weight, up_weight, down_weight, routes, seq_lengths, out_grad,
):
    own = lax.axis_index("expert").astype(jnp.int32).reshape(1)
    gain_one = norm_attn.reshape(1, D)
    gain_two = norm_moe.reshape(1, D)
    shard_rows = D // DP

    shard, half, rows = call(
        prep_kernel,
        [sds((DP, shard_rows, WW), bf16), sds((shard_rows, HALF), bf16), sds((ROWS, PW), bf16)],
        scratch=[pltpu.VMEM((shard_rows, WW), bf16)],
        cost=cost(3),
        in_specs=[SM] + [VM] * 8,
    )(own, query_weight, key_weight, value_weight, router_weight, out_weight, tokens, out_grad, routes)
    pieces = gather_rows(rows)
    weights = lax.all_to_all(shard, "dp", 0, 0, tiled=True).reshape(D, WW)
    out_mine = lax.all_gather(half, "dp", axis=0, tiled=True)

    end_one = seq_lengths[0, 0]
    end_two = end_one + seq_lengths[0, 1]
    place = jnp.arange(GROUP, dtype=jnp.int32)
    start = jnp.where(place >= end_two, end_two, jnp.where(place >= end_one, end_one, 0)).astype(jnp.int32)
    steps = jnp.arange(HD // 2, dtype=f32)
    freq = jnp.exp(steps * (-2.0 * math.log(THETA) / HD))
    angles = (place - start).astype(f32)[:, None] * freq[None, :]
    cos_half, sin_half = jnp.cos(angles), jnp.sin(angles)
    cos_t = jnp.tile(cos_half, (1, 8))
    sin_t = jnp.tile(jnp.concatenate([-sin_half, sin_half], axis=1), (1, 4))
    start = start.reshape(GROUP, 1)

    part = lambda piece, width, at: pl.BlockSpec(
        (piece.shape[0], width), lambda e: (0, at), pipeline_mode=pl.Buffered(1)
    )
    normed_one, qkv, mix, logs = call(
        attend_kernel,
        [sds((GROUP, D), bf16), sds((GROUP, WW), bf16), sds((OWN, ROWS, BLK), bf16), sds((GROUP, 8), f32)],
        cost=cost(12),
        grid=(1,),
        in_specs=[SM] + [part(p, D, 0) for p in pieces] + [VM] * 5,
    )(own, *pieces, weights, gain_one, cos_t, sin_t, start)
    out_mine = gate(out_mine, mix)
    out_other = move(out_mine, SWAP)

    mix_own = lax.all_to_all(mix, "expert", 0, 0, tiled=True)
    hidden, normed_two, mix_flat = call(
        out_kernel,
        [sds((ROWS, D), f32), sds((ROWS, D), bf16), sds((ROWS, D), bf16)],
        cost=cost(4),
        in_specs=[SM] + [VM] * 5,
    )(own, mix_own, out_mine, out_other, tokens, gain_two)
    n_all = lax.all_gather(normed_two, "expert", axis=0, tiled=True)
    mix_flat = gate(mix_flat, n_all)
    mix_all = lax.all_gather(mix_flat, "expert", axis=0, tiled=True)

    whole = lambda *shape: pl.BlockSpec(shape, lambda e: (0,) * len(shape), pipeline_mode=pl.Buffered(1))
    each = lambda *shape: pl.BlockSpec((1,) + shape, lambda e: (e, 0, 0))
    gg, gu, gd, hg, hu, gated, p_slots, slot_rows = call(
        expert_kernel,
        [
            sds((EXP_DEV, D, FFE), bf16), sds((EXP_DEV, D, FFE), bf16), sds((EXP_DEV, FFE, D), bf16),
            sds((EXP_DEV, SLOTS, FFE), bf16), sds((EXP_DEV, SLOTS, FFE), bf16), sds((EXP_DEV, SLOTS, D), bf16),
            sds((EXP_DEV, SLOTS, 128), bf16), sds((EXP_DEV, 8, GROUP), jnp.int32),
        ],
        scratch=[
            pltpu.VMEM((128, GROUP), f32), pltpu.VMEM((SLOTS, D), bf16), pltpu.VMEM((SLOTS, D), bf16),
            pltpu.VMEM((SLOTS, 1), f32), pltpu.VMEM((GROUP, D), bf16), pltpu.VMEM((TOP, GROUP), f32),
        ],
        cost=cost(28),
        grid=(EXP_DEV,),
        in_specs=[SM] + [part(p, D, 1) for p in pieces] + [part(p, 128, 2 * D // 128) for p in pieces] + [
            whole(GROUP, D), whole(D, WW), each(D, FFE), each(D, FFE), each(FFE, D),
        ],
        out_specs=[
            each(D, FFE), each(D, FFE), each(FFE, D), each(SLOTS, FFE), each(SLOTS, FFE), each(SLOTS, D),
            each(SLOTS, 128), each(8, GROUP),
        ],
    )(own, *pieces, *pieces, n_all, weights, gate_weight, up_weight, down_weight)

    down_total, gate_total, up_total = lax.psum((gd, gg, gu), "dp")

    dx_keep, dx_send = call(
        return_kernel,
        [sds((PAIRS, ROWS, XW), bf16)] * 2,
        scratch=[pltpu.VMEM((EXP_DEV, SLOTS, D), bf16)],
        cost=cost(1),
        grid=(EXP_DEV,),
        in_specs=[
            SM, each(SLOTS, FFE), each(SLOTS, FFE), whole(EXP_DEV, SLOTS, 128), whole(EXP_DEV, 8, GROUP),
            each(D, FFE), each(D, FFE),
        ],
        out_specs=[whole(PAIRS, ROWS, XW)] * 2,
    )(own, hg, hu, p_slots, slot_rows, gate_weight, up_weight)
    mix_keep, mix_send = call(
        mixture_kernel, [sds((PAIRS, ROWS, D), bf16)] * 2, cost=cost(5), in_specs=[SM, VM, VM]
    )(own, gated, slot_rows)

    first = pl.BlockSpec((1, ROWS, XW), lambda i: (0, 0, 0))
    first_d = pl.BlockSpec((1, ROWS, D), lambda i: (0, 0, 0))
    dx_parts = scatter_rows(dx_keep, dx_send)
    hidden_grad, moe_gain, send, cols = call(
        hidden_kernel,
        [sds((ROWS, D), f32), sds((1, D), f32), sds((OWN, ROWS, BLK), bf16), sds((OWN, ROWS, WW), bf16)],
        cost=cost(1),
        grid=(1,),
        in_specs=[SM, first] + [VM] * 9,
    )(own, *dx_parts, out_grad, hidden, normed_two, gain_two, weights, out_mine, out_other)
    mix_grad = lax.all_to_all(send, "expert", 0, 0, tiled=True).reshape(GROUP, BLK)
    got = lax.all_to_all(cols, "expert", 0, 0, tiled=True).reshape(GROUP, WW)
    dqkv = call(
        attend_back_kernel,
        sds((GROUP, WW), bf16),
        scratch=[pltpu.VMEM((GROUP, BLK), f32), pltpu.VMEM((GROUP, HD), f32), pltpu.VMEM((GROUP, HD), f32)],
        cost=cost(12),
    )(qkv, logs, mix_grad, cos_t, sin_t, start)
    back_keep, back_send, pay = call(
        weight_kernel,
        [sds((PAIRS, ROWS, D), bf16)] * 2 + [sds((D, 640), bf16)],
        scratch=[pltpu.VMEM((8, D), f32)],
        cost=cost(1),
        in_specs=[SM] + [VM] * 8,
    )(own, normed_one, dqkv, mix_all, got, n_all, moe_gain, gain_one, weights)

    pay_parts = lax.all_to_all(pay.reshape(DP, shard_rows, 640), "dp", 0, 0, tiled=True)
    pay_own, router_total = call(
        sum_kernel, [sds((OWN, shard_rows, 640), bf16), sds((shard_rows, EXPERTS), f32)], cost=cost(1)
    )(pay_parts)
    pay_all = lax.all_to_all(pay_own, "expert", 0, 0, tiled=True)
    query_total, key_total, value_total, out_total, gains = call(
        join_kernel,
        [sds((shard_rows, w), f32) for w in (D, KVH * HD, KVH * HD, D)] + [sds((DP, 8, 128), f32)],
        cost=cost(1),
    )(pay_all)
    gains = lax.all_to_all(gains, "dp", 0, 0, tiled=True)
    gain_attn = gains[:, 0, :shard_rows].reshape(D)
    gain_moe = gains[:, 1, :shard_rows].reshape(D)

    mix_parts = scatter_rows(mix_keep, mix_send)
    layer_out = call(
        layer_kernel, sds((ROWS, D), bf16), cost=cost(1), grid=(1,), in_specs=[first_d, VM, VM, VM]
    )(*mix_parts, hidden)
    back_parts = scatter_rows(back_keep, back_send)
    input_grad = call(
        input_kernel, sds((ROWS, D), bf16), cost=cost(1), grid=(1,), in_specs=[first_d] + [VM] * 5
    )(*back_parts, tokens, gain_one, hidden_grad)
    return (
        layer_out, input_grad, gain_attn, query_total, key_total, value_total, out_total, gain_moe, router_total,
        gate_total.astype(f32), up_total.astype(f32), down_total.astype(f32),
    )


def solution(mesh):
    both, dp, expert = P(("dp", "expert"), None), P("dp", None), P("expert", None, None)
    return jax.shard_map(
        body,
        mesh=mesh,
        in_specs=(both, P(), dp, dp, dp, dp, P(), dp, expert, expert, expert, both, dp, both),
        out_specs=(both, both, P(), dp, dp, dp, dp, P(), dp, expert, expert, expert),
        check_vma=False,
    )
```

```python
import functools
import math

import jax
import jax.numpy as jnp
from jax import lax
from jax.experimental import pallas as pl
from jax.experimental.pallas import tpu as pltpu
from jax.sharding import PartitionSpec as P

QH = 24
KVH = 8
HD = 64
TOP = 8
EXP_DEV = 3
CAP = 56
D = 1536
FFE = 512
ROWS = 128
OWN = 8
GROUP = 1024
DP = 16
EXPERTS = 24
HEADS = 3
QW = HEADS * HD
PAIR = 2 * CAP
PAIRS = OWN // 2
SLOTS = OWN * CAP
BLK = 256
WW = 384
XW = D + 128
CUT = FFE // 2
DOWN_ROWS = FFE // DP
GRAD_ROWS = 3 * (D // DP)
HALF = D // 2
EPS = 1e-06
THETA = 10000.0
VMEM = 60 * 1024 * 1024
f32 = jnp.float32
bf16 = jnp.bfloat16

NN = (((1,), (0,)), ((), ()))
NT = (((1,), (1,)), ((), ()))
TN = (((0,), (0,)), ((), ()))


def mm(a, b, dims=NN):
    return lax.dot_general(a, b, dims, preferred_element_type=f32)


def iota(shape, dim):
    return lax.broadcasted_iota(jnp.int32, shape, dim)


def swap_halves(v):
    lane = iota(v.shape, 1) % HD
    width = v.shape[1]
    ahead = pltpu.roll(v, width - HD // 2, 1)
    behind = pltpu.roll(v, HD // 2, 1)
    return jnp.where(lane < HD // 2, ahead, behind)


def block_mask(start_ref, at, keys):
    place = at + iota((BLK, keys), 0)
    key = iota((BLK, keys), 1)
    first = start_ref[pl.ds(at, BLK), :]
    return (key <= place) & (key >= first)


def turn(v):
    rows, cols = v.shape
    v = jnp.concatenate([v, jnp.zeros((128 - rows, cols), f32)], axis=0)
    if cols < 128:
        v = jnp.concatenate([v, jnp.zeros((128, 128 - cols), f32)], axis=1)
    return jnp.transpose(v)


def prep_kernel(
    own_ref, wq_ref, wk_ref, wv_ref, wr_ref, dy_ref, routes_ref, shard_ref, rows_ref, own_cols
):
    own = own_ref[0]
    rows_ref[:, 0:D] = dy_ref[...]
    rows_ref[:, D:XW] = turn(routes_ref[...].astype(f32)).astype(bf16)
    own_cols[...] = jnp.zeros_like(own_cols)
    for j in range(OWN):

        @pl.when(own == j)
        def _(j=j):
            own_cols[:, 0:QW] = wq_ref[:, j * QW : (j + 1) * QW]
            own_cols[:, QW:BLK] = wk_ref[:, j * HD : (j + 1) * HD]
            own_cols[:, BLK : BLK + HD] = wv_ref[:, j * HD : (j + 1) * HD]

    own_cols[:, BLK + HD : BLK + HD + EXPERTS] = turn(wr_ref[...].astype(f32))[0 : D // DP, 0:EXPERTS].astype(bf16)
    shard_ref[...] = jnp.broadcast_to(own_cols[...][None], shard_ref.shape)


def gate_kernel(in_ref, *refs):
    pass


def owner_of(own, dz, dc):
    return ((own // 2 + dz) % 4) * 2 + (own + dc) % 2


def pieces_of(refs):
    near, up, down, far_a, far_b = range(5)
    for dc in range(2):
        mine = refs[dc * 5 : dc * 5 + 5]
        yield 0, dc, lambda mine=mine: mine[near][...]
        yield 1, dc, lambda mine=mine: mine[down][...]
        yield 3, dc, lambda mine=mine: mine[up][...]
        yield 2, dc, lambda mine=mine: jnp.concatenate([mine[far_a][...], mine[far_b][...]], axis=0)


def whole_pieces_of(refs):
    for dc in range(2):
        for dz, at in ((0, 0), (3, 1), (1, 2), (2, 3)):
            yield dz, dc, lambda at=dc * 4 + at: refs[at][...]


def attend_kernel(own_ref, *refs):
    x_refs, refs = refs[:10], refs[10:]
    w_ref, gain_ref, cos_ref, sin_ref, start_ref, normed_ref, qkv_ref, mix_ref, log_ref = refs
    own = own_ref[0]
    for dz, dc, load in pieces_of(x_refs):
        rows = pl.ds(pl.multiple_of(owner_of(own, dz, dc) * ROWS, ROWS), ROWS)
        x = load().astype(f32)
        scale = lax.rsqrt(jnp.mean(x * x, axis=-1, keepdims=True) + EPS)
        normed_ref[rows, :] = (x * scale * gain_ref[...]).astype(bf16)
    for at in range(0, GROUP, 2 * BLK):
        rows = pl.ds(at, 2 * BLK)
        raw = mm(normed_ref[rows, :], w_ref[...])
        turned = raw[:, :BLK]
        turned = turned * cos_ref[rows, :] + swap_halves(turned) * sin_ref[rows, :]
        qkv_ref[rows, 0:BLK] = turned.astype(bf16)
        qkv_ref[rows, BLK:WW] = raw[:, BLK:WW].astype(bf16)
    for at in range(0, GROUP, BLK):
        rows = pl.ds(at, BLK)
        keys = at + BLK
        seen = block_mask(start_ref, at, keys)
        k_h = qkv_ref[0:keys, QW : QW + HD]
        v_h = qkv_ref[0:keys, BLK : BLK + HD]
        outs = []
        for r in range(HEADS):
            q_h = qkv_ref[rows, r * HD : (r + 1) * HD] * jnp.asarray(HD**-0.5, bf16)
            scores = jnp.where(seen, mm(q_h, k_h, NT), -1e30)
            top = jnp.max(scores, axis=-1, keepdims=True)
            terms = jnp.exp(scores - top)
            total = jnp.sum(terms, axis=-1, keepdims=True)
            prob = (terms / total).astype(bf16)
            outs.append(mm(prob, v_h))
            log_ref[rows, r : r + 1] = top + jnp.log(total)
        block = jnp.concatenate(outs + [jnp.zeros_like(outs[0])], axis=1).astype(bf16)
        mix_ref[at // ROWS] = block[0:ROWS]
        mix_ref[at // ROWS + 1] = block[ROWS:BLK]


def out_kernel(mix_ref, wo_ref, x_ref, gain_ref, hidden_ref, normed_ref, flat_ref):
    for j in range(OWN):
        flat_ref[:, j * QW : (j + 1) * QW] = mix_ref[j, :, 0:QW]
    hidden = x_ref[...].astype(f32) + mm(flat_ref[...], wo_ref[...])
    hidden_ref[...] = hidden
    scale = lax.rsqrt(jnp.mean(hidden * hidden, axis=-1, keepdims=True) + EPS)
    normed_ref[...] = (hidden * scale * gain_ref[...]).astype(bf16)


def router_probs(normed, w_ref):
    logits = mm(normed, w_ref[:, BLK:WW])
    lane = iota(logits.shape, 1)
    real = (lane >= HD) & (lane < HD + EXPERTS)
    logits = jnp.where(real, logits, -1e30)
    terms = jnp.exp(logits - jnp.max(logits, axis=-1, keepdims=True))
    terms = jnp.where(real, terms, 0.0)
    return terms / jnp.sum(terms, axis=-1, keepdims=True)


def pick_rows(slot_row, b):
    row = slot_row[:, b * BLK : (b + 1) * BLK]
    return iota((PAIR, BLK), 0) == row


def slots_kernel(own_ref, *refs):
    slot_ref, d_ref, routes_ref, dy_ref = refs[8:]
    for dz, dc, load in whole_pieces_of(refs[:8]):
        rows = pl.ds(pl.multiple_of(owner_of(own_ref[0], dz, dc) * ROWS, ROWS), ROWS)
        piece = load()
        dy_ref[rows, :] = piece[:, 0:D]
        routes_ref[:, rows] = jnp.transpose(piece[:, D:XW].astype(f32))[0:TOP]
    before = (iota((ROWS, ROWS), 0) < iota((ROWS, ROWS), 1)).astype(f32).astype(bf16)
    for e in range(EXP_DEV):
        own = own_ref[0] * EXP_DEV + e
        chosen = jnp.max((routes_ref[...] == own.astype(f32)).astype(f32), axis=0, keepdims=True)
        ranks = []
        for s in range(OWN):
            part = jnp.broadcast_to(chosen[:, s * ROWS : (s + 1) * ROWS], (8, ROWS)).astype(bf16)
            ranks.append(mm(part, before)[0:1] + float(CAP * (s % 2)))
        rank = jnp.concatenate(ranks, axis=1)
        slot_row = jnp.where(chosen > 0.0, rank, -1.0).astype(jnp.int32)
        slot_ref[e] = jnp.broadcast_to(slot_row, (8, GROUP))
        for b in range(PAIRS):
            pick = pick_rows(slot_row, b).astype(f32).astype(bf16)
            d_ref[e, b * PAIR : (b + 1) * PAIR, :] = mm(pick, dy_ref[b * BLK : (b + 1) * BLK, :]).astype(bf16)


def expert_kernel(own_ref, *refs):
    n_refs, refs = refs[:10], refs[10:]
    w_ref, d_ref, slot_ref, wg_ref, wu_ref, wd_ref, gg_ref, gu_ref, gd_ref, hg_ref, hu_ref, inner_ref, gate_ref = refs[:13]
    prob_ref, x_ref, n_ref = refs[13:]
    e = pl.program_id(0)
    own = own_ref[0] * EXP_DEV + e

    @pl.when(e == 0)
    def _():
        for dz, dc, load in pieces_of(n_refs):
            rows = pl.ds(pl.multiple_of(owner_of(own_ref[0], dz, dc) * ROWS, ROWS), ROWS)
            n_ref[rows, :] = load()
        for at in range(0, GROUP, BLK):
            probs = router_probs(n_ref[at : at + BLK, :], w_ref)
            prob_ref[:, at : at + BLK] = jnp.transpose(probs)

    gate_row = jnp.sum(jnp.where(iota((128, GROUP), 0) == HD + own, prob_ref[...], 0.0), axis=0, keepdims=True)
    slot_row = slot_ref[0, 0:1, :]
    for b in range(PAIRS):
        pick = pick_rows(slot_row, b)
        slots = pl.ds(b * PAIR, PAIR)
        x_ref[slots, :] = mm(pick.astype(f32).astype(bf16), n_ref[b * BLK : (b + 1) * BLK, :]).astype(bf16)
        gate_ref[0, slots, :] = jnp.sum(jnp.where(pick, gate_row[:, b * BLK : (b + 1) * BLK], 0.0), axis=1, keepdims=True)
    x = x_ref[...]
    gate_in = mm(x, wg_ref[0])
    up_in = mm(x, wu_ref[0])
    sig = jax.nn.sigmoid(gate_in)
    silu = gate_in * sig
    inner = (silu * up_in).astype(bf16)
    inner_ref[0] = inner
    gates = gate_ref[0]
    dy = d_ref[0].astype(f32)
    slot_grad = (gates * dy).astype(bf16)
    inner_grad = mm(slot_grad, wd_ref[0], NT)
    hg = (inner_grad * up_in * sig * (1.0 + gate_in * (1.0 - sig))).astype(bf16)
    hu = (inner_grad * silu).astype(bf16)
    hg_ref[0] = hg
    hu_ref[0] = hu
    gd_ref[0] = mm(inner, slot_grad, TN).astype(bf16)
    both = mm(x, jnp.concatenate([hg, hu], axis=1), TN)
    gg_ref[0] = both[:, 0:FFE].astype(bf16)
    gu_ref[0] = both[:, FFE : 2 * FFE].astype(bf16)


def widen_kernel(*refs):
    for in_ref, out_ref in zip(refs[:3], refs[3:]):
        out_ref[...] = in_ref[...].astype(f32)


def split_core(core, both):
    first, second = both[0:ROWS], both[ROWS:BLK]
    return jnp.where(core == 0, first, second), jnp.where(core == 0, second, first)


def scatter_pairs(own, slot_ref, parts):
    for dz in range(PAIRS):
        b = (own // 2 + dz) % PAIRS
        tokens = pl.ds(pl.multiple_of(b * BLK, BLK), BLK)
        slots = pl.ds(pl.multiple_of(b * PAIR, PAIR), PAIR)
        pick = jnp.concatenate(
            [(iota((PAIR, BLK), 0) == slot_ref[k, 0:1, tokens]).astype(f32).astype(bf16) for k in range(EXP_DEV)],
            axis=0,
        )
        for ref, width, at, keep_ref, send_ref in parts:
            values = jnp.concatenate([ref[k, slots, :] for k in range(EXP_DEV)], axis=0)
            keep, send = split_core(own % 2, mm(pick, values, TN))
            keep_ref[dz, :, at : at + width] = keep.astype(bf16)
            send_ref[dz, :, at : at + width] = send.astype(bf16)


def return_kernel(
    own_ref, hg_ref, hu_ref, inner_ref, gate_ref, d_ref, slot_ref, wg_ref, wu_ref, wd_ref,
    keep_ref, send_ref, gated_ref, rows_ref, p_ref,
):
    e = pl.program_id(0)
    own = own_ref[0] * EXP_DEV + e
    rows_ref[e] = (mm(hg_ref[0], wg_ref[0], NT) + mm(hu_ref[0], wu_ref[0], NT)).astype(bf16)
    out = mm(inner_ref[0], wd_ref[0]).astype(bf16).astype(f32)
    gated_ref[0] = (gate_ref[0] * out).astype(bf16)
    p = jnp.sum(d_ref[0].astype(f32) * out, axis=-1, keepdims=True)
    high = p.astype(bf16).astype(f32)
    lane = iota((SLOTS, 128), 1)
    p_ref[e] = jnp.where(lane == HD + own, high, jnp.where(lane == HD + 32 + own, p - high, 0.0)).astype(bf16)

    @pl.when(e == EXP_DEV - 1)
    def _():
        scatter_pairs(
            own_ref[0], slot_ref, ((rows_ref, D, 0, keep_ref, send_ref), (p_ref, 128, D, keep_ref, send_ref))
        )


def tokens_kernel(own_ref, gated_ref, slot_ref, dqkv_ref, w_ref, after_ref, keep_ref, send_ref):
    own = own_ref[0]
    scatter_pairs(own, slot_ref, ((gated_ref, D, D, keep_ref, send_ref),))
    for dz in range(PAIRS):
        b = (own // 2 + dz) % PAIRS
        rows = pl.ds(pl.multiple_of(b * BLK, BLK), BLK)
        keep, send = split_core(own % 2, mm(dqkv_ref[rows, :], w_ref[...], NT))
        keep_ref[dz, :, 0:D] = keep.astype(bf16)
        send_ref[dz, :, 0:D] = send.astype(bf16)


def first_sum_kernel(keep_ref, got_ref, near_ref, one_ref, three_ref, far_a_ref, far_b_ref):
    half = ROWS // 2

    def total(dz, rows):
        return (keep_ref[dz, rows, :].astype(f32) + got_ref[dz, rows, :].astype(f32)).astype(bf16)

    whole = slice(0, ROWS)
    far_a_ref[...] = total(2, slice(0, half))
    far_b_ref[...] = total(2, slice(half, ROWS))
    one_ref[...] = total(1, whole)
    three_ref[...] = total(3, whole)
    near_ref[...] = total(0, whole)


def second_sum_kernel(one_ref, three_ref, up_ref, down_ref, first_ref, last_ref):
    half = ROWS // 2
    first_ref[0:half, :] = (one_ref[0:half, :].astype(f32) + up_ref[...].astype(f32)).astype(bf16)
    first_ref[half:ROWS, :] = one_ref[half:ROWS, :]
    last_ref[0:half, :] = three_ref[0:half, :]
    last_ref[half:ROWS, :] = (three_ref[half:ROWS, :].astype(f32) + down_ref[...].astype(f32)).astype(bf16)


def hidden_kernel(
    part_a, part_b, part_c, dy_ref, hidden_ref, normed_ref, gain_ref, w_ref, wo_ref,
    grad_ref, gain_grad_ref, send_ref, cols_ref, logit_ref,
):
    hidden = hidden_ref[...]
    scale = lax.rsqrt(jnp.mean(hidden * hidden, axis=-1, keepdims=True) + EPS)
    unit = hidden * scale
    total = part_a[...].astype(f32) + part_b[...].astype(f32) + part_c[...].astype(f32)
    tail = total[:, D:XW]
    probs = router_probs(normed_ref[...], w_ref)
    p = tail + pltpu.roll(tail, 128 - 32, 1)
    logit_grad = probs * (p - jnp.sum(p * probs, axis=-1, keepdims=True))
    high = logit_grad.astype(bf16)
    low = (logit_grad - high.astype(f32)).astype(bf16)
    logit_ref[0] = high
    logit_ref[1] = low
    router = w_ref[:, BLK:WW]
    normed_grad = total[:, 0:D] + mm(high, router, NT) + mm(low, router, NT)
    gain_grad_ref[...] = jnp.sum(normed_grad * unit, axis=0, keepdims=True)
    unit_grad = normed_grad * gain_ref[...]
    grad = dy_ref[...].astype(f32) + scale * (unit_grad - unit * jnp.mean(unit_grad * unit, axis=-1, keepdims=True))
    grad_ref[...] = grad
    mix_grad = mm(grad.astype(bf16), wo_ref[...], NT)
    for j in range(OWN):
        cols = slice(j * QW, (j + 1) * QW)
        send_ref[j, :, 0:QW] = mix_grad[:, cols].astype(bf16)
        send_ref[j, :, QW:BLK] = jnp.zeros((ROWS, BLK - QW), bf16)
        cols_ref[j, :, 0:HD] = jnp.zeros((ROWS, HD), bf16)
        cols_ref[j, :, HD:BLK] = grad[:, cols].astype(bf16)


def attend_back_kernel(qkv_ref, log_ref, g_ref, cos_ref, sin_ref, start_ref, dqkv_ref, turn_ref, dk_ref, dv_ref):
    dk_ref[...] = jnp.zeros_like(dk_ref)
    dv_ref[...] = jnp.zeros_like(dv_ref)
    for at in range(0, GROUP, BLK):
        rows = pl.ds(at, BLK)
        keys = at + BLK
        seen = block_mask(start_ref, at, keys)
        k_h = qkv_ref[0:keys, QW : QW + HD]
        v_h = qkv_ref[0:keys, BLK : BLK + HD]
        for r in range(HEADS):
            q_h = qkv_ref[rows, r * HD : (r + 1) * HD] * jnp.asarray(HD**-0.5, bf16)
            g_h = g_ref[rows, r * HD : (r + 1) * HD]
            scores = jnp.where(seen, mm(q_h, k_h, NT), -1e30)
            prob = jnp.exp(scores - log_ref[rows, r : r + 1])
            dv_ref[0:keys, :] += mm(prob.astype(bf16), g_h, TN)
            prob_grad = mm(g_h, v_h, NT)
            delta = jnp.sum(prob_grad * prob, axis=-1, keepdims=True)
            score_grad = (prob * (prob_grad - delta)).astype(bf16)
            turn_ref[rows, r * HD : (r + 1) * HD] = mm(score_grad, k_h) * (HD**-0.5)
            dk_ref[0:keys, :] += mm(score_grad, q_h, TN)
    turn_ref[:, QW : QW + HD] = dk_ref[...]
    for at in range(0, GROUP, BLK):
        rows = pl.ds(at, BLK)
        turned = turn_ref[rows, :]
        turned = turned * cos_ref[rows, :] - swap_halves(turned) * sin_ref[rows, :]
        dqkv_ref[rows, 0:BLK] = turned.astype(bf16)
        dqkv_ref[rows, BLK : BLK + HD] = dv_ref[rows, :].astype(bf16)
        dqkv_ref[rows, BLK + HD : WW] = jnp.zeros((BLK, WW - BLK - HD), bf16)


def pay_kernel(normed_ref, dqkv_ref, mix_ref, got_ref, n_ref, logit_ref, moe_gain_ref, norm_ref, w_ref, pay_ref):
    left = mm(normed_ref[...], dqkv_ref[:, 0:BLK], TN)
    pay_ref[:, 0:BLK] = left.astype(bf16)
    value = mm(normed_ref[...], dqkv_ref[:, BLK:WW], TN)
    out = mm(mix_ref[...], got_ref[...], TN)
    pay_ref[:, BLK : 2 * BLK] = (jnp.concatenate([value, jnp.zeros((D, 128), f32)], axis=1) + out).astype(bf16)
    router = mm(n_ref[...], logit_ref[0], TN) + mm(n_ref[...], logit_ref[1], TN)
    attn_gain = jnp.sum(left * w_ref[:, 0:BLK].astype(f32), axis=1, keepdims=True)
    attn_gain = attn_gain + jnp.sum(value * w_ref[:, BLK:WW].astype(f32), axis=1, keepdims=True)
    gains = jnp.concatenate([1.0 / norm_ref[...], moe_gain_ref[...], jnp.zeros((126, D), f32)], axis=0)
    gains = jnp.transpose(gains)
    rows = D // DP
    lane = iota((rows, 128), 1)
    attn_gain, moe_gain = attn_gain * gains[:, 0:1], gains[:, 1:2]
    both = jnp.zeros((rows, 128), f32)
    for i in range(DP):
        part = slice(i * rows, (i + 1) * rows)
        both = jnp.where(lane == i, attn_gain[part], jnp.where(lane == DP + i, moe_gain[part], both))
    for i in range(DP):
        part = slice(i * rows, (i + 1) * rows)
        pay_ref[part, 2 * BLK : 2 * BLK + 128] = jnp.where(lane >= HD, router[part], both).astype(bf16)


def input_kernel(part_a, part_b, part_c, x_ref, gain_ref, hidden_grad_ref, hidden_ref, out_ref, layer_ref):
    x = x_ref[...].astype(f32)
    scale = lax.rsqrt(jnp.mean(x * x, axis=-1, keepdims=True) + EPS)
    unit = x * scale
    total = part_a[...].astype(f32) + part_b[...].astype(f32) + part_c[...].astype(f32)
    unit_grad = total[:, 0:D] * gain_ref[...]
    out_ref[...] = (
        hidden_grad_ref[...] + scale * (unit_grad - unit * jnp.mean(unit_grad * unit, axis=-1, keepdims=True))
    ).astype(bf16)
    layer_ref[...] = (hidden_ref[...] + total[:, D : 2 * D]).astype(bf16)


def sum_kernel(part_ref, after_ref, sum_ref):
    total = part_ref[0].astype(f32)
    for s in range(1, DP):
        total = total + part_ref[s].astype(f32)
    sum_ref[...] = jnp.broadcast_to(total.astype(bf16)[None], sum_ref.shape)


def join_kernel(part_ref, q_ref, k_ref, v_ref, o_ref, router_ref, gain_ref):
    gains = jnp.zeros((D // DP, 128), f32)
    for j in range(OWN):
        part = part_ref[j].astype(f32)
        q_ref[:, j * QW : (j + 1) * QW] = part[:, 0:QW]
        k_ref[:, j * HD : (j + 1) * HD] = part[:, QW:BLK]
        v_ref[:, j * HD : (j + 1) * HD] = part[:, BLK : BLK + HD]
        o_ref[:, j * QW : (j + 1) * QW] = part[:, BLK + HD : 2 * BLK]
        gains = gains + part[:, 2 * BLK : 2 * BLK + 128]
    router_ref[...] = gains[:, HD : HD + EXPERTS]
    gains = jnp.concatenate([gains, jnp.zeros((128 - D // DP, 128), f32)], axis=0)
    gain_ref[...] = jnp.transpose(gains)[0 : 2 * DP]


def sds(shape, dtype):
    return jax.ShapeDtypeStruct(shape, dtype)


def call(kernel, outs, scratch=(), cost=None, **grid):
    return pl.pallas_call(
        kernel,
        out_shape=outs,
        scratch_shapes=list(scratch),
        compiler_params=pltpu.CompilerParams(vmem_limit_bytes=VMEM),
        cost_estimate=cost,
        **grid,
    )


def cost(micros):
    return pl.CostEstimate(flops=int(micros * 1.15e9), bytes_accessed=1024, transcendentals=0)


VM = pl.BlockSpec(memory_space=pltpu.VMEM)
SM = pl.BlockSpec(memory_space=pltpu.SMEM)
ANY = pl.BlockSpec(memory_space=pl.ANY)


def along_z(step):
    return [(i, ((i // 2 + step) % 4) * 2 + i % 2) for i in range(OWN)]


UP, DOWN, SWAP = along_z(1), along_z(-1), [(i, i ^ 1) for i in range(OWN)]


def move(value, pairs):
    return lax.ppermute(value, "expert", pairs)


def gate(value, *after):
    return pl.pallas_call(
        gate_kernel,
        out_shape=sds(value.shape, value.dtype),
        in_specs=[ANY] * (1 + len(after)),
        out_specs=ANY,
        input_output_aliases={0: 0},
        compiler_params=pltpu.CompilerParams(vmem_limit_bytes=VMEM),
        cost_estimate=cost(0.5),
    )(value, *after)


def ring_rows(value, after=()):
    half = value.shape[0] // 2
    up, down = move(value, UP), move(value, DOWN)
    if after:
        up = gate(up, *after)
    far_a, far_b = move(up[:half], UP), move(down[half:], DOWN)
    return [value, up, down, far_a, far_b]


def swap_rows(mine):
    return mine + [move(piece, SWAP) for piece in mine]


def scatter_rows(keep, send):
    width = keep.shape[2]
    whole, half = sds((ROWS, width), bf16), sds((ROWS // 2, width), bf16)
    near, one, three, far_a, far_b = call(first_sum_kernel, [whole] * 3 + [half] * 2, cost=cost(0.1))(
        keep, move(send, SWAP)
    )
    first, last = call(second_sum_kernel, [whole] * 2, cost=cost(1))(one, three, move(far_a, UP), move(far_b, DOWN))
    return (near, move(first, UP), move(last, DOWN)), far_a


def body(
    tokens, norm_attn, query_weight, key_weight, value_weight, out_weight, norm_moe, router_weight,
    gate_weight, up_weight, down_weight, routes, seq_lengths, out_grad,
):
    own = lax.axis_index("expert").astype(jnp.int32).reshape(1)
    gain_one = norm_attn.reshape(1, D)
    gain_two = norm_moe.reshape(1, D)
    shard_rows = D // DP

    shard, rows = call(
        prep_kernel,
        [sds((DP, shard_rows, WW), bf16), sds((ROWS, XW), bf16)],
        scratch=[pltpu.VMEM((shard_rows, WW), bf16)],
        cost=cost(3),
        in_specs=[SM] + [VM] * 6,
    )(own, query_weight, key_weight, value_weight, router_weight.T, out_grad, routes.T)
    weights = lax.all_to_all(shard, "dp", 0, 0, tiled=True).reshape(D, WW)
    out_full = lax.all_gather(out_weight, "dp", axis=0, tiled=True)
    end_one = seq_lengths[0, 0]
    end_two = end_one + seq_lengths[0, 1]
    place = jnp.arange(GROUP, dtype=jnp.int32)
    start = jnp.where(place >= end_two, end_two, jnp.where(place >= end_one, end_one, 0)).astype(jnp.int32)
    steps = jnp.arange(HD // 2, dtype=f32)
    freq = jnp.exp(steps * (-2.0 * math.log(THETA) / HD))
    angles = (place - start).astype(f32)[:, None] * freq[None, :]
    cos_half, sin_half = jnp.cos(angles), jnp.sin(angles)
    cos_t = jnp.tile(cos_half, (1, 8))
    sin_t = jnp.tile(jnp.concatenate([-sin_half, sin_half], axis=1), (1, 4))
    start = start.reshape(GROUP, 1)
    x_ring = ring_rows(tokens)
    x_ring[3] = gate(x_ring[3], cos_t, sin_t, start)
    x_pieces = swap_rows(x_ring)
    dy_rows = gate(rows, x_ring[1], x_ring[2])
    dy_up, dy_down = move(dy_rows, UP), move(dy_rows, DOWN)
    dy_ring = [dy_rows, dy_up, dy_down, move(dy_up, UP)]

    part = lambda piece, width, at: pl.BlockSpec(
        (piece.shape[0], width), lambda e: (0, at), pipeline_mode=pl.Buffered(1)
    )
    normed_one, qkv, mix, logs = call(
        attend_kernel,
        [sds((GROUP, D), bf16), sds((GROUP, WW), bf16), sds((OWN, ROWS, BLK), bf16), sds((GROUP, 8), f32)],
        cost=cost(12),
        in_specs=[SM] + [VM] * 15,
    )(own, *x_pieces, weights, gain_one, cos_t, sin_t, start)

    mix_own = lax.all_to_all(gate(mix, dy_ring[2], dy_ring[3]), "expert", 0, 0, tiled=True)
    dy_pieces = swap_rows(dy_ring)
    hidden, normed_two, mix_flat = call(
        out_kernel,
        [sds((ROWS, D), f32), sds((ROWS, D), bf16), sds((ROWS, D), bf16)],
        cost=cost(4),
    )(mix_own, out_full, tokens, gain_two)
    slot_rows, d_slots = call(
        slots_kernel,
        [sds((EXP_DEV, 8, GROUP), jnp.int32), sds((EXP_DEV, SLOTS, D), bf16)],
        scratch=[pltpu.VMEM((TOP, GROUP), f32), pltpu.VMEM((GROUP, D), bf16)],
        cost=cost(6),
        in_specs=[SM] + [VM] * 8,
    )(own, *dy_pieces)
    n_pieces = swap_rows(ring_rows(normed_two, (slot_rows,)))
    mix_flat = gate(mix_flat, n_pieces[3], n_pieces[4])
    mix_all = lax.all_gather(mix_flat, "expert", axis=0, tiled=True)

    whole = lambda *shape: pl.BlockSpec(shape, lambda e: (0,) * len(shape), pipeline_mode=pl.Buffered(1))
    each = lambda *shape: pl.BlockSpec((1,) + shape, lambda e: (e, 0, 0))
    gg, gu, gd, hg, hu, inner, gates = call(
        expert_kernel,
        [
            sds((EXP_DEV, D, FFE), bf16), sds((EXP_DEV, D, FFE), bf16), sds((EXP_DEV, FFE, D), bf16),
            sds((EXP_DEV, SLOTS, FFE), bf16), sds((EXP_DEV, SLOTS, FFE), bf16), sds((EXP_DEV, SLOTS, FFE), bf16),
            sds((EXP_DEV, SLOTS, 1), f32),
        ],
        scratch=[
            pltpu.VMEM((128, GROUP), f32), pltpu.VMEM((SLOTS, D), bf16), pltpu.VMEM((GROUP, D), bf16),
        ],
        cost=cost(28),
        grid=(EXP_DEV,),
        in_specs=[
            SM, *[whole(*p.shape) for p in n_pieces], whole(D, WW), each(SLOTS, D), each(8, GROUP),
            each(D, FFE), each(D, FFE), each(FFE, D),
        ],
        out_specs=[
            each(D, FFE), each(D, FFE), each(FFE, D), each(SLOTS, FFE), each(SLOTS, FFE), each(SLOTS, FFE), each(SLOTS, 1),
        ],
    )(own, *n_pieces, weights, d_slots, slot_rows, gate_weight, up_weight, down_weight)

    gate_part, up_part, down_part = lax.psum((gate(gg, mix_all), gu, gd), "dp")

    dx_keep, dx_send, gated = call(
        return_kernel,
        [sds((PAIRS, ROWS, XW), bf16)] * 2 + [sds((EXP_DEV, SLOTS, D), bf16)],
        scratch=[pltpu.VMEM((EXP_DEV, SLOTS, D), bf16), pltpu.VMEM((EXP_DEV, SLOTS, 128), bf16)],
        cost=cost(1),
        grid=(EXP_DEV,),
        in_specs=[
            SM, each(SLOTS, FFE), each(SLOTS, FFE), each(SLOTS, FFE), each(SLOTS, 1), each(SLOTS, D),
            whole(EXP_DEV, 8, GROUP), each(D, FFE), each(D, FFE), each(FFE, D),
        ],
        out_specs=[whole(PAIRS, ROWS, XW)] * 2 + [each(SLOTS, D)],
    )(own, hg, hu, inner, gates, d_slots, slot_rows, gate_weight, up_weight, down_weight)

    dx_parts, _ = scatter_rows(dx_keep, dx_send)
    hidden_grad, moe_gain, send, cols, logit_grads = call(
        hidden_kernel,
        [sds((ROWS, D), f32), sds((1, D), f32), sds((OWN, ROWS, BLK), bf16), sds((OWN, ROWS, BLK), bf16),
            sds((2, ROWS, 128), bf16)],
        cost=cost(1),
    )(*dx_parts, out_grad, hidden, normed_two, gain_two, weights, out_full)
    mix_grad = lax.all_to_all(send, "expert", 0, 0, tiled=True).reshape(GROUP, BLK)
    got = lax.all_to_all(cols, "expert", 0, 0, tiled=True).reshape(GROUP, BLK)
    dqkv = call(
        attend_back_kernel,
        sds((GROUP, WW), bf16),
        scratch=[pltpu.VMEM((GROUP, BLK), f32), pltpu.VMEM((GROUP, HD), f32), pltpu.VMEM((GROUP, HD), f32)],
        cost=cost(12),
    )(qkv, logs, mix_grad, cos_t, sin_t, start)
    pay = call(pay_kernel, sds((D, 640), bf16), cost=cost(1))(
        normed_one, dqkv, mix_all, got, normed_two, logit_grads, moe_gain, gain_one, weights
    )
    pay_parts = lax.all_to_all(pay.reshape(DP, shard_rows, 640), "dp", 0, 0, tiled=True)
    rows_keep, rows_send = call(
        tokens_kernel, [sds((PAIRS, ROWS, 2 * D), bf16)] * 2, cost=cost(0.1), in_specs=[SM] + [VM] * 4 + [ANY]
    )(own, gated, slot_rows, dqkv, weights, pay)
    rows_parts, rows_first = scatter_rows(rows_keep, rows_send)
    pay_own = call(
        sum_kernel, sds((OWN, shard_rows, 640), bf16), cost=cost(1), in_specs=[VM, ANY]
    )(pay_parts, rows_first)
    pay_all = lax.all_to_all(pay_own, "expert", 0, 0, tiled=True)
    query_total, key_total, value_total, out_total, router_total, gains = call(
        join_kernel,
        [sds((shard_rows, w), f32) for w in (D, KVH * HD, KVH * HD, D, EXPERTS)] + [sds((2 * DP, 128), f32)],
        cost=cost(0.02),
    )(pay_all)
    gain_attn = gains[0:DP, :shard_rows].reshape(D)
    gain_moe = gains[DP:, :shard_rows].reshape(D)
    input_grad, layer_out = call(input_kernel, [sds((ROWS, D), bf16)] * 2, cost=cost(1))(
        *rows_parts, tokens, gain_one, hidden_grad, hidden
    )
    cut = lambda rows, cols: pl.BlockSpec((1, rows, cols), lambda e, h: (e, h, 0))
    widths = [cut(D // 2, FFE), cut(D // 2, FFE), cut(FFE // 2, D)]
    gate_total, up_total, down_total = call(
        widen_kernel,
        [sds((EXP_DEV, D, FFE), f32), sds((EXP_DEV, D, FFE), f32), sds((EXP_DEV, FFE, D), f32)],
        cost=cost(12),
        grid=(EXP_DEV, 2),
        in_specs=widths,
        out_specs=widths,
    )(gate_part, up_part, down_part)
    return (
        layer_out, input_grad, gain_attn, query_total, key_total, value_total, out_total, gain_moe, router_total,
        gate_total, up_total, down_total,
    )


def solution(mesh):
    both, dp, expert = P(("dp", "expert"), None), P("dp", None), P("expert", None, None)
    return jax.shard_map(
        body,
        mesh=mesh,
        in_specs=(both, P(), dp, dp, dp, dp, P(), dp, expert, expert, expert, both, dp, both),
        out_specs=(both, both, P(), dp, dp, dp, dp, P(), dp, expert, expert, expert),
        check_vma=False,
    )
```

```python
import functools
import math

import jax
import jax.numpy as jnp
from jax import lax
from jax.experimental import pallas as pl
from jax.experimental.pallas import tpu as pltpu
from jax.sharding import PartitionSpec as P

QH = 24
KVH = 8
HD = 64
TOP = 8
EXP_DEV = 3
CAP = 56
D = 1536
FFE = 512
ROWS = 128
OWN = 8
GROUP = 1024
DP = 16
EXPERTS = 24
HEADS = 3
QW = HEADS * HD
PAIR = 2 * CAP
PAIRS = OWN // 2
SLOTS = OWN * CAP
BLK = 256
WW = 384
XW = D + 128
CUT = FFE // 2
DOWN_ROWS = FFE // DP
GRAD_ROWS = 3 * (D // DP)
HALF = D // 2
EPS = 1e-06
THETA = 10000.0
VMEM = 64 * 1024 * 1024 - 65536
f32 = jnp.float32
bf16 = jnp.bfloat16

NN = (((1,), (0,)), ((), ()))
NT = (((1,), (1,)), ((), ()))
TN = (((0,), (0,)), ((), ()))


def mm(a, b, dims=NN):
    return lax.dot_general(a, b, dims, preferred_element_type=f32)


def iota(shape, dim):
    return lax.broadcasted_iota(jnp.int32, shape, dim)


def twice(v):
    return jnp.concatenate([v, v], axis=1)


def swap_halves(v):
    lane = iota(v.shape, 1) % HD
    width = v.shape[1]
    ahead = pltpu.roll(v, width - HD // 2, 1)
    behind = pltpu.roll(v, HD // 2, 1)
    return jnp.where(lane < HD // 2, ahead, behind)


def block_mask(start_ref, at, keys):
    place = at + iota((BLK, keys), 0)
    key = iota((BLK, keys), 1)
    first = start_ref[pl.ds(at, BLK), :]
    return (key <= place) & (key >= first)


def turn(v):
    rows, cols = v.shape
    v = jnp.concatenate([v, jnp.zeros((128 - rows, cols), f32)], axis=0)
    if cols < 128:
        v = jnp.concatenate([v, jnp.zeros((128, 128 - cols), f32)], axis=1)
    return jnp.transpose(v)


def prep_kernel(
    own_ref, wq_ref, wk_ref, wv_ref, wr_ref, dy_ref, routes_ref, shard_ref, rows_ref, own_cols
):
    own = own_ref[0]
    rows_ref[:, 0:D] = dy_ref[...]
    rows_ref[:, D:XW] = turn(routes_ref[...].astype(f32)).astype(bf16)
    own_cols[...] = jnp.zeros_like(own_cols)
    for j in range(OWN):

        @pl.when(own == j)
        def _(j=j):
            own_cols[:, 0:QW] = wq_ref[:, j * QW : (j + 1) * QW]
            own_cols[:, QW:BLK] = wk_ref[:, j * HD : (j + 1) * HD]
            own_cols[:, BLK : BLK + HD] = wv_ref[:, j * HD : (j + 1) * HD]

    own_cols[:, BLK + HD : BLK + HD + EXPERTS] = turn(wr_ref[...].astype(f32))[0 : D // DP, 0:EXPERTS].astype(bf16)
    shard_ref[...] = jnp.broadcast_to(own_cols[...][None], shard_ref.shape)


def gate_kernel(in_ref, *refs):
    pass


def owner_of(own, dz, dc):
    return ((own // 2 + dz) % 4) * 2 + (own + dc) % 2


def pieces_of(refs):
    near, up, down, far_a, far_b = range(5)
    for dc in range(2):
        mine = refs[dc * 5 : dc * 5 + 5]
        yield 0, dc, lambda mine=mine: mine[near][...]
        yield 1, dc, lambda mine=mine: mine[down][...]
        yield 3, dc, lambda mine=mine: mine[up][...]
        yield 2, dc, lambda mine=mine: jnp.concatenate([mine[far_a][...], mine[far_b][...]], axis=0)


def whole_pieces_of(refs):
    for dc in range(2):
        for dz, at in ((0, 0), (3, 1), (1, 2), (2, 3)):
            yield dz, dc, lambda at=dc * 4 + at: refs[at][...]


def attend_kernel(own_ref, *refs):
    x_refs, refs = refs[:10], refs[10:]
    w_ref, gain_ref, cos_ref, sin_ref, start_ref, normed_ref, qkv_ref, mix_ref, log_ref = refs
    own = own_ref[0]
    for dz, dc, load in pieces_of(x_refs):
        rows = pl.ds(pl.multiple_of(owner_of(own, dz, dc) * ROWS, ROWS), ROWS)
        x = load().astype(f32)
        scale = lax.rsqrt(jnp.mean(x * x, axis=-1, keepdims=True) + EPS)
        normed = (x * scale * gain_ref[...]).astype(bf16)
        normed_ref[rows, :] = normed
        raw = mm(normed, w_ref[...])
        turned = raw[:, :BLK]
        turned = turned * twice(cos_ref[rows, :]) + swap_halves(turned) * twice(sin_ref[rows, :])
        qkv_ref[rows, 0:BLK] = turned.astype(bf16)
        qkv_ref[rows, BLK:WW] = raw[:, BLK:WW].astype(bf16)
    for at in range(0, GROUP, BLK):
        rows = pl.ds(at, BLK)
        keys = at + BLK
        seen = block_mask(start_ref, at, keys)
        k_h = qkv_ref[0:keys, QW : QW + HD]
        v_h = qkv_ref[0:keys, BLK : BLK + HD]
        outs = []
        for r in range(HEADS):
            q_h = qkv_ref[rows, r * HD : (r + 1) * HD] * jnp.asarray(HD**-0.5, bf16)
            scores = jnp.where(seen, mm(q_h, k_h, NT), -1e30)
            top = jnp.max(scores, axis=-1, keepdims=True)
            terms = jnp.exp(scores - top)
            total = jnp.sum(terms, axis=-1, keepdims=True)
            prob = (terms / total).astype(bf16)
            outs.append(mm(prob, v_h))
            log_ref[rows, r : r + 1] = top + jnp.log(total)
        block = jnp.concatenate(outs + [jnp.zeros_like(outs[0])], axis=1).astype(bf16)
        mix_ref[at // ROWS] = block[0:ROWS]
        mix_ref[at // ROWS + 1] = block[ROWS:BLK]


def out_kernel(mix_ref, wo_ref, x_ref, gain_ref, hidden_ref, normed_ref, flat_ref):
    for j in range(OWN):
        flat_ref[:, j * QW : (j + 1) * QW] = mix_ref[j, :, 0:QW]
    hidden = x_ref[...].astype(f32) + mm(flat_ref[...], wo_ref[...])
    hidden_ref[...] = hidden
    scale = lax.rsqrt(jnp.mean(hidden * hidden, axis=-1, keepdims=True) + EPS)
    normed_ref[...] = (hidden * scale * gain_ref[...]).astype(bf16)


def router_probs(normed, w_ref):
    logits = mm(normed, w_ref[:, BLK:WW])
    lane = iota(logits.shape, 1)
    real = (lane >= HD) & (lane < HD + EXPERTS)
    logits = jnp.where(real, logits, -1e30)
    terms = jnp.exp(logits - jnp.max(logits, axis=-1, keepdims=True))
    terms = jnp.where(real, terms, 0.0)
    return terms / jnp.sum(terms, axis=-1, keepdims=True)


def pick_rows(slot_row, b):
    row = slot_row[:, b * BLK : (b + 1) * BLK]
    return iota((PAIR, BLK), 0) == row


def slots_kernel(own_ref, *refs):
    slot_ref, d_ref, routes_ref, dy_ref = refs[8:]
    for dz, dc, load in whole_pieces_of(refs[:8]):
        rows = pl.ds(pl.multiple_of(owner_of(own_ref[0], dz, dc) * ROWS, ROWS), ROWS)
        piece = load()
        dy_ref[rows, :] = piece[:, 0:D]
        routes_ref[:, rows] = jnp.transpose(piece[:, D:XW].astype(f32))[0:TOP]
    before = (iota((ROWS, ROWS), 0) < iota((ROWS, ROWS), 1)).astype(f32).astype(bf16)
    for e in range(EXP_DEV):
        own = own_ref[0] * EXP_DEV + e
        chosen = jnp.max((routes_ref[...] == own.astype(f32)).astype(f32), axis=0, keepdims=True)
        ranks = []
        for s in range(OWN):
            part = jnp.broadcast_to(chosen[:, s * ROWS : (s + 1) * ROWS], (8, ROWS)).astype(bf16)
            ranks.append(mm(part, before)[0:1] + float(CAP * (s % 2)))
        rank = jnp.concatenate(ranks, axis=1)
        slot_row = jnp.where(chosen > 0.0, rank, -1.0).astype(jnp.int32)
        slot_ref[e] = jnp.broadcast_to(slot_row, (8, GROUP))
        for b in range(PAIRS):
            pick = pick_rows(slot_row, b).astype(f32).astype(bf16)
            d_ref[e, b * PAIR : (b + 1) * PAIR, :] = mm(pick, dy_ref[b * BLK : (b + 1) * BLK, :]).astype(bf16)


def expert_kernel(own_ref, *refs):
    n_refs, refs = refs[:10], refs[10:]
    w_ref, d_ref, slot_ref, wg_ref, wu_ref, wd_ref, grad_ref, hg_ref, hu_ref, inner_ref, gate_ref = refs[:11]
    prob_ref, x_ref, n_ref = refs[11:]
    e = pl.program_id(0)
    own = own_ref[0] * EXP_DEV + e

    @pl.when(e == 0)
    def _():
        for dz, dc, load in pieces_of(n_refs):
            rows = pl.ds(pl.multiple_of(owner_of(own_ref[0], dz, dc) * ROWS, ROWS), ROWS)
            n_ref[rows, :] = load()
        for at in range(0, GROUP, BLK):
            probs = router_probs(n_ref[at : at + BLK, :], w_ref)
            prob_ref[:, at : at + BLK] = jnp.transpose(probs)

    gate_row = jnp.sum(jnp.where(iota((128, GROUP), 0) == HD + own, prob_ref[...], 0.0), axis=0, keepdims=True)
    slot_row = slot_ref[0, 0:1, :]
    for b in range(PAIRS):
        pick = pick_rows(slot_row, b)
        slots = pl.ds(b * PAIR, PAIR)
        x_ref[slots, :] = mm(pick.astype(f32).astype(bf16), n_ref[b * BLK : (b + 1) * BLK, :]).astype(bf16)
        gate_ref[0, slots, :] = jnp.sum(jnp.where(pick, gate_row[:, b * BLK : (b + 1) * BLK], 0.0), axis=1, keepdims=True)
    x = x_ref[...]
    gate_in = mm(x, wg_ref[0])
    up_in = mm(x, wu_ref[0])
    sig = jax.nn.sigmoid(gate_in)
    silu = gate_in * sig
    inner = (silu * up_in).astype(bf16)
    inner_ref[0] = inner
    gates = gate_ref[0]
    dy = d_ref[0].astype(f32)
    slot_grad = (gates * dy).astype(bf16)
    inner_grad = mm(slot_grad, wd_ref[0], NT)
    hg = (inner_grad * up_in * sig * (1.0 + gate_in * (1.0 - sig))).astype(bf16)
    hu = (inner_grad * silu).astype(bf16)
    hg_ref[0] = hg
    hu_ref[0] = hu
    down = mm(inner, slot_grad, TN).astype(bf16)
    for c in range(3):
        grad_ref[0, 2, c * FFE : (c + 1) * FFE, :] = down[:, c * FFE : (c + 1) * FFE]
    both = mm(x, jnp.concatenate([hg, hu], axis=1), TN)
    grad_ref[0, 0] = both[:, 0:FFE].astype(bf16)
    grad_ref[0, 1] = both[:, FFE : 2 * FFE].astype(bf16)


def widen_kernel(both_ref, down_part_ref, gate_ref, up_ref, down_ref):
    gate_ref[0] = both_ref[0, 0].astype(f32)
    up_ref[0] = both_ref[0, 1].astype(f32)
    for c in range(3):
        down_ref[0, :, c * FFE : (c + 1) * FFE] = down_part_ref[0, 0, c].astype(f32)


def split_core(core, both):
    first, second = both[0:ROWS], both[ROWS:BLK]
    return jnp.where(core == 0, first, second), jnp.where(core == 0, second, first)


def scatter_pairs(own, slot_ref, parts):
    for dz in range(PAIRS):
        b = (own // 2 + dz) % PAIRS
        tokens = pl.ds(pl.multiple_of(b * BLK, BLK), BLK)
        slots = pl.ds(pl.multiple_of(b * PAIR, PAIR), PAIR)
        pick = jnp.concatenate(
            [(iota((PAIR, BLK), 0) == slot_ref[k, 0:1, tokens]).astype(f32).astype(bf16) for k in range(EXP_DEV)],
            axis=0,
        )
        for ref, width, at, keep_ref, send_ref in parts:
            values = jnp.concatenate([ref[k, slots, :] for k in range(EXP_DEV)], axis=0)
            keep, send = split_core(own % 2, mm(pick, values, TN))
            keep_ref[dz, :, at : at + width] = keep.astype(bf16)
            send_ref[dz, :, at : at + width] = send.astype(bf16)


def return_kernel(
    own_ref, hg_ref, hu_ref, inner_ref, gate_ref, d_ref, slot_ref, wg_ref, wu_ref, wd_ref,
    keep_ref, send_ref, gated_ref, rows_ref, p_ref,
):
    e = pl.program_id(0)
    own = own_ref[0] * EXP_DEV + e
    rows_ref[e] = (mm(hg_ref[0], wg_ref[0], NT) + mm(hu_ref[0], wu_ref[0], NT)).astype(bf16)
    out = mm(inner_ref[0], wd_ref[0]).astype(bf16).astype(f32)
    gated_ref[0] = (gate_ref[0] * out).astype(bf16)
    p = jnp.sum(d_ref[0].astype(f32) * out, axis=-1, keepdims=True)
    high = p.astype(bf16).astype(f32)
    lane = iota((SLOTS, 128), 1)
    p_ref[e] = jnp.where(lane == HD + own, high, jnp.where(lane == HD + 32 + own, p - high, 0.0)).astype(bf16)

    @pl.when(e == EXP_DEV - 1)
    def _():
        scatter_pairs(
            own_ref[0], slot_ref, ((rows_ref, D, 0, keep_ref, send_ref), (p_ref, 128, D, keep_ref, send_ref))
        )


def tokens_kernel(own_ref, gated_ref, slot_ref, dqkv_ref, w_ref, after_ref, keep_ref, send_ref):
    own = own_ref[0]
    scatter_pairs(own, slot_ref, ((gated_ref, D, D, keep_ref, send_ref),))
    for dz in range(PAIRS):
        b = (own // 2 + dz) % PAIRS
        rows = pl.ds(pl.multiple_of(b * BLK, BLK), BLK)
        keep, send = split_core(own % 2, mm(dqkv_ref[rows, :], w_ref[...], NT))
        keep_ref[dz, :, 0:D] = keep.astype(bf16)
        send_ref[dz, :, 0:D] = send.astype(bf16)


def first_sum_kernel(keep_ref, got_ref, near_ref, one_ref, three_ref, far_a_ref, far_b_ref):
    half = ROWS // 2

    def total(dz, rows):
        return (keep_ref[dz, rows, :].astype(f32) + got_ref[dz, rows, :].astype(f32)).astype(bf16)

    whole = slice(0, ROWS)
    far_a_ref[...] = total(2, slice(0, half))
    far_b_ref[...] = total(2, slice(half, ROWS))
    one_ref[...] = total(1, whole)
    three_ref[...] = total(3, whole)
    near_ref[...] = total(0, whole)


def second_sum_kernel(one_ref, three_ref, up_ref, down_ref, first_ref, last_ref):
    half = ROWS // 2
    first_ref[0:half, :] = (one_ref[0:half, :].astype(f32) + up_ref[...].astype(f32)).astype(bf16)
    first_ref[half:ROWS, :] = one_ref[half:ROWS, :]
    last_ref[0:half, :] = three_ref[0:half, :]
    last_ref[half:ROWS, :] = (three_ref[half:ROWS, :].astype(f32) + down_ref[...].astype(f32)).astype(bf16)


def hidden_kernel(
    part_a, part_b, part_c, dy_ref, hidden_ref, normed_ref, gain_ref, w_ref, wo_ref,
    grad_ref, gain_grad_ref, send_ref, cols_ref, logit_ref,
):
    hidden = hidden_ref[...]
    scale = lax.rsqrt(jnp.mean(hidden * hidden, axis=-1, keepdims=True) + EPS)
    unit = hidden * scale
    total = part_a[...].astype(f32) + part_b[...].astype(f32) + part_c[...].astype(f32)
    tail = total[:, D:XW]
    probs = router_probs(normed_ref[...], w_ref)
    p = tail + pltpu.roll(tail, 128 - 32, 1)
    logit_grad = probs * (p - jnp.sum(p * probs, axis=-1, keepdims=True))
    high = logit_grad.astype(bf16)
    low = (logit_grad - high.astype(f32)).astype(bf16)
    logit_ref[0] = high
    logit_ref[1] = low
    router = w_ref[:, BLK:WW]
    normed_grad = total[:, 0:D] + mm(high, router, NT) + mm(low, router, NT)
    gain_grad_ref[...] = jnp.sum(normed_grad * unit, axis=0, keepdims=True)
    unit_grad = normed_grad * gain_ref[...]
    grad = dy_ref[...].astype(f32) + scale * (unit_grad - unit * jnp.mean(unit_grad * unit, axis=-1, keepdims=True))
    grad_ref[...] = grad
    mix_grad = mm(grad.astype(bf16), wo_ref[...], NT)
    for j in range(OWN):
        cols = slice(j * QW, (j + 1) * QW)
        send_ref[j, :, 0:QW] = mix_grad[:, cols].astype(bf16)
        send_ref[j, :, QW:BLK] = jnp.zeros((ROWS, BLK - QW), bf16)
        cols_ref[j, :, 0:HD] = jnp.zeros((ROWS, HD), bf16)
        cols_ref[j, :, HD:BLK] = grad[:, cols].astype(bf16)


def attend_back_kernel(qkv_ref, log_ref, g_ref, cos_ref, sin_ref, start_ref, dqkv_ref, turn_ref, dk_ref, dv_ref):
    dk_ref[...] = jnp.zeros_like(dk_ref)
    dv_ref[...] = jnp.zeros_like(dv_ref)
    for at in range(0, GROUP, BLK):
        rows = pl.ds(at, BLK)
        keys = at + BLK
        seen = block_mask(start_ref, at, keys)
        k_h = qkv_ref[0:keys, QW : QW + HD]
        v_h = qkv_ref[0:keys, BLK : BLK + HD]
        for r in range(HEADS):
            q_h = qkv_ref[rows, r * HD : (r + 1) * HD] * jnp.asarray(HD**-0.5, bf16)
            g_h = g_ref[rows, r * HD : (r + 1) * HD]
            scores = jnp.where(seen, mm(q_h, k_h, NT), -1e30)
            prob = jnp.exp(scores - log_ref[rows, r : r + 1])
            dv_ref[0:keys, :] += mm(prob.astype(bf16), g_h, TN)
            prob_grad = mm(g_h, v_h, NT)
            delta = jnp.sum(prob_grad * prob, axis=-1, keepdims=True)
            score_grad = (prob * (prob_grad - delta)).astype(bf16)
            turn_ref[rows, r * HD : (r + 1) * HD] = mm(score_grad, k_h) * (HD**-0.5)
            dk_ref[0:keys, :] += mm(score_grad, q_h, TN)
    turn_ref[:, QW : QW + HD] = dk_ref[...]
    for at in range(0, GROUP, BLK):
        rows = pl.ds(at, BLK)
        turned = turn_ref[rows, :]
        turned = turned * twice(cos_ref[rows, :]) - swap_halves(turned) * twice(sin_ref[rows, :])
        dqkv_ref[rows, 0:BLK] = turned.astype(bf16)
        dqkv_ref[rows, BLK : BLK + HD] = dv_ref[rows, :].astype(bf16)
        dqkv_ref[rows, BLK + HD : WW] = jnp.zeros((BLK, WW - BLK - HD), bf16)


def pay_kernel(normed_ref, dqkv_ref, mix_ref, got_ref, n_ref, logit_ref, moe_gain_ref, norm_ref, w_ref, pay_ref):
    left = mm(normed_ref[...], dqkv_ref[:, 0:BLK], TN)
    pay_ref[:, 0:BLK] = left.astype(bf16)
    value = mm(normed_ref[...], dqkv_ref[:, BLK:WW], TN)
    out = mm(mix_ref[...], got_ref[...], TN)
    pay_ref[:, BLK : 2 * BLK] = (jnp.concatenate([value, jnp.zeros((D, 128), f32)], axis=1) + out).astype(bf16)
    router = mm(n_ref[...], logit_ref[0], TN) + mm(n_ref[...], logit_ref[1], TN)
    attn_gain = jnp.sum(left * w_ref[:, 0:BLK].astype(f32), axis=1, keepdims=True)
    attn_gain = attn_gain + jnp.sum(value * w_ref[:, BLK:WW].astype(f32), axis=1, keepdims=True)
    gains = jnp.concatenate([1.0 / norm_ref[...], moe_gain_ref[...], jnp.zeros((126, D), f32)], axis=0)
    gains = jnp.transpose(gains)
    rows = D // DP
    lane = iota((rows, 128), 1)
    attn_gain, moe_gain = attn_gain * gains[:, 0:1], gains[:, 1:2]
    both = jnp.zeros((rows, 128), f32)
    for i in range(DP):
        part = slice(i * rows, (i + 1) * rows)
        both = jnp.where(lane == i, attn_gain[part], jnp.where(lane == DP + i, moe_gain[part], both))
    for i in range(DP):
        part = slice(i * rows, (i + 1) * rows)
        pay_ref[part, 2 * BLK : 2 * BLK + 128] = jnp.where(lane >= HD, router[part], both).astype(bf16)


def input_kernel(part_a, part_b, part_c, x_ref, gain_ref, hidden_grad_ref, hidden_ref, out_ref, layer_ref):
    x = x_ref[...].astype(f32)
    scale = lax.rsqrt(jnp.mean(x * x, axis=-1, keepdims=True) + EPS)
    unit = x * scale
    total = part_a[...].astype(f32) + part_b[...].astype(f32) + part_c[...].astype(f32)
    unit_grad = total[:, 0:D] * gain_ref[...]
    out_ref[...] = (
        hidden_grad_ref[...] + scale * (unit_grad - unit * jnp.mean(unit_grad * unit, axis=-1, keepdims=True))
    ).astype(bf16)
    layer_ref[...] = (hidden_ref[...] + total[:, D : 2 * D]).astype(bf16)


def sum_kernel(part_ref, after_ref, sum_ref):
    total = part_ref[0].astype(f32)
    for s in range(1, part_ref.shape[0]):
        total = total + part_ref[s].astype(f32)
    sum_ref[...] = jnp.broadcast_to(total.astype(bf16)[None], sum_ref.shape)


def join_kernel(part_ref, q_ref, k_ref, v_ref, o_ref, router_ref, gain_ref):
    gains = jnp.zeros((D // DP, 128), f32)
    for j in range(OWN):
        part = part_ref[j].astype(f32)
        q_ref[:, j * QW : (j + 1) * QW] = part[:, 0:QW]
        k_ref[:, j * HD : (j + 1) * HD] = part[:, QW:BLK]
        v_ref[:, j * HD : (j + 1) * HD] = part[:, BLK : BLK + HD]
        o_ref[:, j * QW : (j + 1) * QW] = part[:, BLK + HD : 2 * BLK]
        gains = gains + part[:, 2 * BLK : 2 * BLK + 128]
    router_ref[...] = gains[:, HD : HD + EXPERTS]
    gains = jnp.concatenate([gains, jnp.zeros((128 - D // DP, 128), f32)], axis=0)
    gain_ref[...] = jnp.transpose(gains)[0 : 2 * DP]


def sds(shape, dtype):
    return jax.ShapeDtypeStruct(shape, dtype)


def call(kernel, outs, scratch=(), cost=None, **grid):
    return pl.pallas_call(
        kernel,
        out_shape=outs,
        scratch_shapes=list(scratch),
        compiler_params=pltpu.CompilerParams(vmem_limit_bytes=VMEM),
        cost_estimate=cost,
        **grid,
    )


def cost(micros):
    return pl.CostEstimate(flops=int(micros * 1.15e9), bytes_accessed=1024, transcendentals=0)


VM = pl.BlockSpec(memory_space=pltpu.VMEM)
SM = pl.BlockSpec(memory_space=pltpu.SMEM)
ANY = pl.BlockSpec(memory_space=pl.ANY)


def along_z(step):
    return [(i, ((i // 2 + step) % 4) * 2 + i % 2) for i in range(OWN)]


X_GROUPS = [[y, 4 + y, 8 + y, 12 + y] for y in range(4)]
Y_GROUPS = [[4 * x + y for y in range(4)] for x in range(4)]
UP, DOWN, SWAP = along_z(1), along_z(-1), [(i, i ^ 1) for i in range(OWN)]


def move(value, pairs):
    return lax.ppermute(value, "expert", pairs)


def gate(value, *after):
    return pl.pallas_call(
        gate_kernel,
        out_shape=sds(value.shape, value.dtype),
        in_specs=[ANY] * (1 + len(after)),
        out_specs=ANY,
        input_output_aliases={0: 0},
        compiler_params=pltpu.CompilerParams(vmem_limit_bytes=VMEM),
        cost_estimate=cost(0.5),
    )(value, *after)


def ring_rows(value, after=()):
    half = value.shape[0] // 2
    up, down = move(value, UP), move(value, DOWN)
    if after:
        up = gate(up, *after)
    far_a, far_b = move(up[:half], UP), move(down[half:], DOWN)
    return [value, up, down, far_a, far_b]


def swap_rows(mine):
    return mine + [move(piece, SWAP) for piece in mine]


def scatter_rows(keep, send):
    width = keep.shape[2]
    whole, half = sds((ROWS, width), bf16), sds((ROWS // 2, width), bf16)
    near, one, three, far_a, far_b = call(first_sum_kernel, [whole] * 3 + [half] * 2, cost=cost(0.1))(
        keep, move(send, SWAP)
    )
    first, last = call(second_sum_kernel, [whole] * 2, cost=cost(1))(one, three, move(far_a, UP), move(far_b, DOWN))
    return (near, move(first, UP), move(last, DOWN)), far_a


def body(
    tokens, norm_attn, query_weight, key_weight, value_weight, out_weight, norm_moe, router_weight,
    gate_weight, up_weight, down_weight, routes, seq_lengths, out_grad,
):
    own = lax.axis_index("expert").astype(jnp.int32).reshape(1)
    gain_one = norm_attn.reshape(1, D)
    gain_two = norm_moe.reshape(1, D)
    shard_rows = D // DP

    shard, rows = call(
        prep_kernel,
        [sds((DP, shard_rows, WW), bf16), sds((ROWS, XW), bf16)],
        scratch=[pltpu.VMEM((shard_rows, WW), bf16)],
        cost=cost(3),
        in_specs=[SM] + [VM] * 6,
    )(own, query_weight, key_weight, value_weight, router_weight.T, out_grad, routes.T)
    weights = lax.all_to_all(shard, "dp", 0, 0, tiled=True).reshape(D, WW)
    out_full = lax.all_gather(out_weight, "dp", axis=0, tiled=True)
    end_one = seq_lengths[0, 0]
    end_two = end_one + seq_lengths[0, 1]
    place = jnp.arange(GROUP, dtype=jnp.int32)
    start = jnp.where(place >= end_two, end_two, jnp.where(place >= end_one, end_one, 0)).astype(jnp.int32)
    steps = jnp.arange(HD // 2, dtype=f32)
    freq = jnp.exp(steps * (-2.0 * math.log(THETA) / HD))
    angles = (place - start).astype(f32)[:, None] * freq[None, :]
    cos_half, sin_half = jnp.cos(angles), jnp.sin(angles)
    cos_t = jnp.tile(cos_half, (1, 4))
    sin_t = jnp.tile(jnp.concatenate([-sin_half, sin_half], axis=1), (1, 2))
    start = start.reshape(GROUP, 1)
    x_ring = ring_rows(tokens)
    x_ring[1] = gate(x_ring[1], cos_t, sin_t, start, gain_one, gain_two)
    x_pieces = swap_rows(x_ring)
    dy_rows = rows
    dy_up, dy_down = move(dy_rows, UP), move(dy_rows, DOWN)
    dy_ring = [dy_rows, dy_up, dy_down, move(dy_up, UP)]

    part = lambda piece, width, at: pl.BlockSpec(
        (piece.shape[0], width), lambda e: (0, at), pipeline_mode=pl.Buffered(1)
    )
    normed_one, qkv, mix, logs = call(
        attend_kernel,
        [sds((GROUP, D), bf16), sds((GROUP, WW), bf16), sds((OWN, ROWS, BLK), bf16), sds((GROUP, 8), f32)],
        cost=cost(12),
        in_specs=[SM] + [VM] * 15,
    )(own, *x_pieces, weights, gain_one, cos_t, sin_t, start)

    mix_own = lax.all_to_all(gate(mix, dy_ring[2], dy_ring[3]), "expert", 0, 0, tiled=True)
    dy_pieces = swap_rows(dy_ring)
    hidden, normed_two, mix_flat = call(
        out_kernel,
        [sds((ROWS, D), f32), sds((ROWS, D), bf16), sds((ROWS, D), bf16)],
        cost=cost(4),
    )(mix_own, out_full, tokens, gain_two)
    slot_rows, d_slots = call(
        slots_kernel,
        [sds((EXP_DEV, 8, GROUP), jnp.int32), sds((EXP_DEV, SLOTS, D), bf16)],
        scratch=[pltpu.VMEM((TOP, GROUP), f32), pltpu.VMEM((GROUP, D), bf16)],
        cost=cost(6),
        in_specs=[SM] + [VM] * 8,
    )(own, *dy_pieces)
    n_pieces = swap_rows(ring_rows(normed_two, (slot_rows,)))
    mix_flat = gate(mix_flat, n_pieces[1], n_pieces[2])
    mix_all = lax.all_gather(mix_flat, "expert", axis=0, tiled=True)

    whole = lambda *shape: pl.BlockSpec(shape, lambda e: (0,) * len(shape), pipeline_mode=pl.Buffered(1))
    each = lambda *shape: pl.BlockSpec((1,) + shape, lambda e: (e, 0, 0))
    grads, hg, hu, inner, gates = call(
        expert_kernel,
        [
            sds((EXP_DEV, 3, D, FFE), bf16), sds((EXP_DEV, SLOTS, FFE), bf16), sds((EXP_DEV, SLOTS, FFE), bf16), sds((EXP_DEV, SLOTS, FFE), bf16),
            sds((EXP_DEV, SLOTS, 1), f32),
        ],
        scratch=[
            pltpu.VMEM((128, GROUP), f32), pltpu.VMEM((SLOTS, D), bf16), pltpu.VMEM((GROUP, D), bf16),
        ],
        cost=cost(28),
        grid=(EXP_DEV,),
        in_specs=[
            SM, *[whole(*p.shape) for p in n_pieces], whole(D, WW), each(SLOTS, D), each(8, GROUP),
            each(D, FFE), each(D, FFE), each(FFE, D),
        ],
        out_specs=[
            pl.BlockSpec((1, 3, D, FFE), lambda e: (e, 0, 0, 0)),
            each(SLOTS, FFE), each(SLOTS, FFE), each(SLOTS, FFE), each(SLOTS, 1),
        ],
    )(own, *n_pieces, weights, d_slots, slot_rows, gate_weight, up_weight, down_weight)

    grad_sums = lax.psum(gate(grads, mix_all).reshape(EXP_DEV * 3 * D, FFE), "dp")

    dx_keep, dx_send, gated = call(
        return_kernel,
        [sds((PAIRS, ROWS, XW), bf16)] * 2 + [sds((EXP_DEV, SLOTS, D), bf16)],
        scratch=[pltpu.VMEM((EXP_DEV, SLOTS, D), bf16), pltpu.VMEM((EXP_DEV, SLOTS, 128), bf16)],
        cost=cost(1),
        grid=(EXP_DEV,),
        in_specs=[
            SM, each(SLOTS, FFE), each(SLOTS, FFE), each(SLOTS, FFE), each(SLOTS, 1), each(SLOTS, D),
            whole(EXP_DEV, 8, GROUP), each(D, FFE), each(D, FFE), each(FFE, D),
        ],
        out_specs=[whole(PAIRS, ROWS, XW)] * 2 + [each(SLOTS, D)],
    )(own, hg, hu, inner, gates, d_slots, slot_rows, gate_weight, up_weight, down_weight)

    dx_parts, _ = scatter_rows(dx_keep, dx_send)
    hidden_grad, moe_gain, send, cols, logit_grads = call(
        hidden_kernel,
        [sds((ROWS, D), f32), sds((1, D), f32), sds((OWN, ROWS, BLK), bf16), sds((OWN, ROWS, BLK), bf16),
            sds((2, ROWS, 128), bf16)],
        cost=cost(1),
    )(*dx_parts, out_grad, hidden, normed_two, gain_two, weights, out_full)
    mix_grad = lax.all_to_all(send, "expert", 0, 0, tiled=True).reshape(GROUP, BLK)
    got = lax.all_to_all(cols, "expert", 0, 0, tiled=True).reshape(GROUP, BLK)
    dqkv = call(
        attend_back_kernel,
        sds((GROUP, WW), bf16),
        scratch=[pltpu.VMEM((GROUP, BLK), f32), pltpu.VMEM((GROUP, HD), f32), pltpu.VMEM((GROUP, HD), f32)],
        cost=cost(12),
    )(qkv, logs, mix_grad, cos_t, sin_t, start)
    pay = call(pay_kernel, sds((D, 640), bf16), cost=cost(1))(
        normed_one, dqkv, mix_all, got, normed_two, logit_grads, moe_gain, gain_one, weights
    )
    pay_parts = lax.all_to_all(pay.reshape(4, D // 4, 640), "dp", 0, 0, tiled=True, axis_index_groups=X_GROUPS)
    rows_keep, rows_send = call(
        tokens_kernel, [sds((PAIRS, ROWS, 2 * D), bf16)] * 2, cost=cost(0.1), in_specs=[SM] + [VM] * 4 + [ANY]
    )(own, gated, slot_rows, dqkv, weights, pay)
    rows_parts, rows_first = scatter_rows(rows_keep, rows_send)
    pay_line = call(
        sum_kernel, sds((1, D // 4, 640), bf16), cost=cost(0.1), in_specs=[VM, ANY]
    )(pay_parts, rows_first)
    pay_parts = lax.all_to_all(
        pay_line.reshape(4, shard_rows, 640), "dp", 0, 0, tiled=True, axis_index_groups=Y_GROUPS
    )
    pay_own = call(
        sum_kernel, sds((OWN, shard_rows, 640), bf16), cost=cost(0.1), in_specs=[VM, ANY]
    )(pay_parts, pay_line)
    pay_all = lax.all_to_all(pay_own, "expert", 0, 0, tiled=True)
    query_total, key_total, value_total, out_total, router_total, gains = call(
        join_kernel,
        [sds((shard_rows, w), f32) for w in (D, KVH * HD, KVH * HD, D, EXPERTS)] + [sds((2 * DP, 128), f32)],
        cost=cost(0.02),
    )(pay_all)
    gain_attn = gains[0:DP, :shard_rows].reshape(D)
    gain_moe = gains[DP:, :shard_rows].reshape(D)
    input_grad, layer_out = call(input_kernel, [sds((ROWS, D), bf16)] * 2, cost=cost(1))(
        *rows_parts, tokens, gain_one, hidden_grad, hidden
    )
    cut = lambda rows, cols: pl.BlockSpec((1, rows, cols), lambda e, h: (e, h, 0))
    widths = [cut(D // 2, FFE), cut(D // 2, FFE), cut(FFE // 2, D)]
    gate_total, up_total, down_total = call(
        widen_kernel,
        [sds((EXP_DEV, D, FFE), f32), sds((EXP_DEV, D, FFE), f32), sds((EXP_DEV, FFE, D), f32)],
        cost=cost(12),
        grid=(EXP_DEV, 2),
        in_specs=[
            pl.BlockSpec((1, 2, D // 2, FFE), lambda e, h: (e, 0, h, 0)),
            pl.BlockSpec((1, 1, 3, FFE // 2, FFE), lambda e, h: (e, 2, 0, h, 0)),
        ],
        out_specs=widths,
    )(grad_sums.reshape(EXP_DEV, 3, D, FFE), grad_sums.reshape(EXP_DEV, 3, 3, FFE, FFE))
    return (
        layer_out, input_grad, gain_attn, query_total, key_total, value_total, out_total, gain_moe, router_total,
        gate_total, up_total, down_total,
    )


def solution(mesh):
    both, dp, expert = P(("dp", "expert"), None), P("dp", None), P("expert", None, None)
    return jax.shard_map(
        body,
        mesh=mesh,
        in_specs=(both, P(), dp, dp, dp, dp, P(), dp, expert, expert, expert, both, dp, both),
        out_specs=(both, both, P(), dp, dp, dp, dp, P(), dp, expert, expert, expert),
        check_vma=False,
    )
```

```python
import functools
import math

import jax
import jax.numpy as jnp
from jax import lax
from jax.experimental import pallas as pl
from jax.experimental.pallas import tpu as pltpu
from jax.sharding import PartitionSpec as P

QH = 24
KVH = 8
HD = 64
TOP = 8
EXP_DEV = 3
CAP = 56
D = 1536
FFE = 512
ROWS = 128
OWN = 8
GROUP = 1024
DP = 16
EXPERTS = 24
HEADS = 3
QW = HEADS * HD
PAIR = 2 * CAP
PAIRS = OWN // 2
SLOTS = OWN * CAP
BLK = 256
WW = 384
XW = D + 128
CUT = FFE // 2
DOWN_ROWS = FFE // DP
GRAD_ROWS = 3 * (D // DP)
HALF = D // 2
EPS = 1e-06
THETA = 10000.0
VMEM = 64 * 1024 * 1024 - 65536
f32 = jnp.float32
bf16 = jnp.bfloat16

NN = (((1,), (0,)), ((), ()))
NT = (((1,), (1,)), ((), ()))
TN = (((0,), (0,)), ((), ()))


def mm(a, b, dims=NN):
    return lax.dot_general(a, b, dims, preferred_element_type=f32)


def iota(shape, dim):
    return lax.broadcasted_iota(jnp.int32, shape, dim)


def twice(v):
    return jnp.concatenate([v, v], axis=1)


def swap_halves(v):
    lane = iota(v.shape, 1) % HD
    width = v.shape[1]
    ahead = pltpu.roll(v, width - HD // 2, 1)
    behind = pltpu.roll(v, HD // 2, 1)
    return jnp.where(lane < HD // 2, ahead, behind)


def block_mask(start_ref, at, keys):
    place = at + iota((BLK, keys), 0)
    key = iota((BLK, keys), 1)
    first = start_ref[pl.ds(at, BLK), :]
    return (key <= place) & (key >= first)


def turn(v):
    rows, cols = v.shape
    v = jnp.concatenate([v, jnp.zeros((128 - rows, cols), f32)], axis=0)
    if cols < 128:
        v = jnp.concatenate([v, jnp.zeros((128, 128 - cols), f32)], axis=1)
    return jnp.transpose(v)


def prep_kernel(
    own_ref, wq_ref, wk_ref, wv_ref, wr_ref, dy_ref, routes_ref, shard_ref, rows_ref, own_cols
):
    own = own_ref[0]
    rows_ref[:, 0:D] = dy_ref[...]
    rows_ref[:, D:XW] = turn(routes_ref[...].astype(f32)).astype(bf16)
    own_cols[...] = jnp.zeros_like(own_cols)
    for j in range(OWN):

        @pl.when(own == j)
        def _(j=j):
            own_cols[:, 0:QW] = wq_ref[:, j * QW : (j + 1) * QW]
            own_cols[:, QW:BLK] = wk_ref[:, j * HD : (j + 1) * HD]
            own_cols[:, BLK : BLK + HD] = wv_ref[:, j * HD : (j + 1) * HD]

    own_cols[:, BLK + HD : BLK + HD + EXPERTS] = turn(wr_ref[...].astype(f32))[0 : D // DP, 0:EXPERTS].astype(bf16)
    shard_ref[...] = jnp.broadcast_to(own_cols[...][None], shard_ref.shape)


def gate_kernel(in_ref, *refs):
    pass


def owner_of(own, dz, dc):
    return ((own // 2 + dz) % 4) * 2 + (own + dc) % 2


def pieces_of(refs):
    near, up, down, far_a, far_b = range(5)
    for dc in range(2):
        mine = refs[dc * 5 : dc * 5 + 5]
        yield 0, dc, lambda mine=mine: mine[near][...]
        yield 1, dc, lambda mine=mine: mine[down][...]
        yield 3, dc, lambda mine=mine: mine[up][...]
        yield 2, dc, lambda mine=mine: jnp.concatenate([mine[far_a][...], mine[far_b][...]], axis=0)


def whole_pieces_of(refs):
    for dc in range(2):
        for dz, at in ((0, 0), (3, 1), (1, 2), (2, 3)):
            yield dz, dc, lambda at=dc * 4 + at: refs[at][...]


def attend_kernel(own_ref, *refs):
    x_refs, refs = refs[:10], refs[10:]
    w_ref, gain_ref, cos_ref, sin_ref, start_ref, normed_ref, qkv_ref, mix_ref, log_ref = refs
    own = own_ref[0]
    for dz, dc, load in pieces_of(x_refs):
        rows = pl.ds(pl.multiple_of(owner_of(own, dz, dc) * ROWS, ROWS), ROWS)
        x = load().astype(f32)
        scale = lax.rsqrt(jnp.mean(x * x, axis=-1, keepdims=True) + EPS)
        normed = (x * scale * gain_ref[...]).astype(bf16)
        normed_ref[rows, :] = normed
        raw = mm(normed, w_ref[...])
        turned = raw[:, :BLK]
        turned = turned * twice(cos_ref[rows, :]) + swap_halves(turned) * twice(sin_ref[rows, :])
        qkv_ref[rows, 0:BLK] = turned.astype(bf16)
        qkv_ref[rows, BLK:WW] = raw[:, BLK:WW].astype(bf16)
    for at in range(0, GROUP, BLK):
        rows = pl.ds(at, BLK)
        keys = at + BLK
        seen = block_mask(start_ref, at, keys)
        k_h = qkv_ref[0:keys, QW : QW + HD]
        v_h = qkv_ref[0:keys, BLK : BLK + HD]
        outs = []
        for r in range(HEADS):
            q_h = qkv_ref[rows, r * HD : (r + 1) * HD] * jnp.asarray(HD**-0.5, bf16)
            scores = jnp.where(seen, mm(q_h, k_h, NT), -1e30)
            top = jnp.max(scores, axis=-1, keepdims=True)
            terms = jnp.exp(scores - top)
            total = jnp.sum(terms, axis=-1, keepdims=True)
            prob = (terms / total).astype(bf16)
            outs.append(mm(prob, v_h))
            log_ref[rows, r : r + 1] = top + jnp.log(total)
        block = jnp.concatenate(outs + [jnp.zeros_like(outs[0])], axis=1).astype(bf16)
        mix_ref[at // ROWS] = block[0:ROWS]
        mix_ref[at // ROWS + 1] = block[ROWS:BLK]


def out_kernel(mix_ref, wo_ref, x_ref, gain_ref, hidden_ref, normed_ref, flat_ref):
    for j in range(OWN):
        flat_ref[:, j * QW : (j + 1) * QW] = mix_ref[j, :, 0:QW]
    hidden = x_ref[...].astype(f32) + mm(flat_ref[...], wo_ref[...])
    hidden_ref[...] = hidden
    scale = lax.rsqrt(jnp.mean(hidden * hidden, axis=-1, keepdims=True) + EPS)
    normed_ref[...] = (hidden * scale * gain_ref[...]).astype(bf16)


def router_probs(normed, w_ref):
    logits = mm(normed, w_ref[:, -128:])
    lane = iota(logits.shape, 1)
    real = (lane >= HD) & (lane < HD + EXPERTS)
    logits = jnp.where(real, logits, -1e30)
    terms = jnp.exp(logits - jnp.max(logits, axis=-1, keepdims=True))
    terms = jnp.where(real, terms, 0.0)
    return terms / jnp.sum(terms, axis=-1, keepdims=True)


def pick_rows(slot_row, b):
    row = slot_row[:, b * BLK : (b + 1) * BLK]
    return iota((PAIR, BLK), 0) == row


def slots_kernel(own_ref, *refs):
    slot_ref, d_ref, routes_ref, dy_ref = refs[8:]
    for dz, dc, load in whole_pieces_of(refs[:8]):
        rows = pl.ds(pl.multiple_of(owner_of(own_ref[0], dz, dc) * ROWS, ROWS), ROWS)
        piece = load()
        dy_ref[rows, :] = piece[:, 0:D]
        routes_ref[:, rows] = jnp.transpose(piece[:, D:XW].astype(f32))[0:TOP]
    before = (iota((ROWS, ROWS), 0) < iota((ROWS, ROWS), 1)).astype(f32).astype(bf16)
    for e in range(EXP_DEV):
        own = own_ref[0] * EXP_DEV + e
        chosen = jnp.max((routes_ref[...] == own.astype(f32)).astype(f32), axis=0, keepdims=True)
        ranks = []
        for s in range(OWN):
            part = jnp.broadcast_to(chosen[:, s * ROWS : (s + 1) * ROWS], (8, ROWS)).astype(bf16)
            ranks.append(mm(part, before)[0:1] + float(CAP * (s % 2)))
        rank = jnp.concatenate(ranks, axis=1)
        slot_row = jnp.where(chosen > 0.0, rank, -1.0).astype(jnp.int32)
        slot_ref[e] = jnp.broadcast_to(slot_row, (8, GROUP))
        for b in range(PAIRS):
            pick = pick_rows(slot_row, b).astype(f32).astype(bf16)
            d_ref[e, b * PAIR : (b + 1) * PAIR, :] = mm(pick, dy_ref[b * BLK : (b + 1) * BLK, :]).astype(bf16)


def expert_kernel(own_ref, *refs):
    n_refs, refs = refs[:10], refs[10:]
    w_ref, d_ref, slot_ref, wg_ref, wu_ref, wd_ref, grad_ref, hg_ref, hu_ref, inner_ref, gate_ref = refs[:11]
    prob_ref, x_ref, n_ref = refs[11:]
    e = pl.program_id(0)
    own = own_ref[0] * EXP_DEV + e

    @pl.when(e == 0)
    def _():
        for dz, dc, load in pieces_of(n_refs):
            rows = pl.ds(pl.multiple_of(owner_of(own_ref[0], dz, dc) * ROWS, ROWS), ROWS)
            n_ref[rows, :] = load()
        for at in range(0, GROUP, BLK):
            probs = router_probs(n_ref[at : at + BLK, :], w_ref)
            prob_ref[:, at : at + BLK] = jnp.transpose(probs)

    gate_row = jnp.sum(jnp.where(iota((128, GROUP), 0) == HD + own, prob_ref[...], 0.0), axis=0, keepdims=True)
    slot_row = slot_ref[0, 0:1, :]
    for b in range(PAIRS):
        pick = pick_rows(slot_row, b)
        slots = pl.ds(b * PAIR, PAIR)
        x_ref[slots, :] = mm(pick.astype(f32).astype(bf16), n_ref[b * BLK : (b + 1) * BLK, :]).astype(bf16)
        gate_ref[0, slots, :] = jnp.sum(jnp.where(pick, gate_row[:, b * BLK : (b + 1) * BLK], 0.0), axis=1, keepdims=True)
    x = x_ref[...]
    gate_in = mm(x, wg_ref[0])
    up_in = mm(x, wu_ref[0])
    sig = jax.nn.sigmoid(gate_in)
    silu = gate_in * sig
    inner = (silu * up_in).astype(bf16)
    inner_ref[0] = inner
    gates = gate_ref[0]
    dy = d_ref[0].astype(f32)
    slot_grad = (gates * dy).astype(bf16)
    inner_grad = mm(slot_grad, wd_ref[0], NT)
    hg = (inner_grad * up_in * sig * (1.0 + gate_in * (1.0 - sig))).astype(bf16)
    hu = (inner_grad * silu).astype(bf16)
    hg_ref[0] = hg
    hu_ref[0] = hu
    down = mm(inner, slot_grad, TN).astype(bf16)
    for c in range(3):
        grad_ref[0, 2, c * FFE : (c + 1) * FFE, :] = down[:, c * FFE : (c + 1) * FFE]
    both = mm(x, jnp.concatenate([hg, hu], axis=1), TN)
    grad_ref[0, 0] = both[:, 0:FFE].astype(bf16)
    grad_ref[0, 1] = both[:, FFE : 2 * FFE].astype(bf16)


def widen_kernel(part_ref, gate_ref, up_ref, down_ref, in_buf, out_buf, in_sems, out_sems):
    slots, long = in_buf.shape[0], D // 2

    def moves(n):
        e, m, h = n // 6, n // 2 % 3, n % 2
        s = n % slots
        if m < 2:
            rows = pl.ds(h * long, long)
            out_ref = (gate_ref, up_ref)[m]
            return (
                [pltpu.make_async_copy(part_ref.at[e, m, rows, :], in_buf.at[s], in_sems.at[s, 0])],
                [pltpu.make_async_copy(out_buf.at[s], out_ref.at[e, rows, :], out_sems.at[s, 0])],
            )
        size = FFE // 2
        ins, outs = [], []
        for c in range(3):
            here, rows = pl.ds(c * size, size), pl.ds(c * FFE + h * size, size)
            ins.append(pltpu.make_async_copy(part_ref.at[e, m, rows, :], in_buf.at[s, here, :], in_sems.at[s, c]))
            outs.append(
                pltpu.make_async_copy(
                    out_buf.at[s, here, :],
                    down_ref.at[e, pl.ds(h * size, size), pl.ds(c * FFE, FFE)],
                    out_sems.at[s, c],
                )
            )
        return ins, outs

    steps = [moves(n) for n in range(6 * EXP_DEV)]
    for ins, _ in steps[: slots - 1]:
        for copy in ins:
            copy.start()
    for n, (ins, outs) in enumerate(steps):
        if n + slots - 1 < len(steps):
            for copy in steps[n + slots - 1][0]:
                copy.start()
        for copy in ins:
            copy.wait()
        if n >= slots:
            for copy in steps[n - slots][1]:
                copy.wait()
        out_buf[n % slots] = in_buf[n % slots].astype(f32)
        for copy in outs:
            copy.start()
    for _, outs in steps[-slots:]:
        for copy in outs:
            copy.wait()


def split_core(core, both):
    first, second = both[0:ROWS], both[ROWS:BLK]
    return jnp.where(core == 0, first, second), jnp.where(core == 0, second, first)


def scatter_pairs(own, slot_ref, parts):
    for dz in range(PAIRS):
        b = (own // 2 + dz) % PAIRS
        tokens = pl.ds(pl.multiple_of(b * BLK, BLK), BLK)
        slots = pl.ds(pl.multiple_of(b * PAIR, PAIR), PAIR)
        pick = jnp.concatenate(
            [(iota((PAIR, BLK), 0) == slot_ref[k, 0:1, tokens]).astype(f32).astype(bf16) for k in range(EXP_DEV)],
            axis=0,
        )
        for ref, width, at, keep_ref, send_ref in parts:
            values = jnp.concatenate([ref[k, slots, :] for k in range(EXP_DEV)], axis=0)
            keep, send = split_core(own % 2, mm(pick, values, TN))
            keep_ref[dz, :, at : at + width] = keep.astype(bf16)
            send_ref[dz, :, at : at + width] = send.astype(bf16)


def return_kernel(
    own_ref, hg_ref, hu_ref, inner_ref, gate_ref, d_ref, slot_ref, wg_ref, wu_ref, wd_ref,
    keep_ref, send_ref, gated_ref, rows_ref, p_ref,
):
    e = pl.program_id(0)
    own = own_ref[0] * EXP_DEV + e
    rows_ref[e] = (mm(hg_ref[0], wg_ref[0], NT) + mm(hu_ref[0], wu_ref[0], NT)).astype(bf16)
    out = mm(inner_ref[0], wd_ref[0]).astype(bf16).astype(f32)
    gated_ref[0] = (gate_ref[0] * out).astype(bf16)
    p = jnp.sum(d_ref[0].astype(f32) * out, axis=-1, keepdims=True)
    high = p.astype(bf16).astype(f32)
    lane = iota((SLOTS, 128), 1)
    p_ref[e] = jnp.where(lane == HD + own, high, jnp.where(lane == HD + 32 + own, p - high, 0.0)).astype(bf16)

    @pl.when(e == EXP_DEV - 1)
    def _():
        scatter_pairs(
            own_ref[0], slot_ref, ((rows_ref, D, 0, keep_ref, send_ref), (p_ref, 128, D, keep_ref, send_ref))
        )


def tokens_kernel(own_ref, gated_ref, slot_ref, dqkv_ref, w_ref, after_ref, keep_ref, send_ref):
    own = own_ref[0]
    scatter_pairs(own, slot_ref, ((gated_ref, D, D, keep_ref, send_ref),))
    for dz in range(PAIRS):
        b = (own // 2 + dz) % PAIRS
        rows = pl.ds(pl.multiple_of(b * BLK, BLK), BLK)
        keep, send = split_core(own % 2, mm(dqkv_ref[rows, :], w_ref[...], NT))
        keep_ref[dz, :, 0:D] = keep.astype(bf16)
        send_ref[dz, :, 0:D] = send.astype(bf16)


def first_sum_kernel(keep_ref, got_ref, near_ref, one_ref, three_ref, far_a_ref, far_b_ref):
    half = ROWS // 2

    def total(dz, rows):
        return (keep_ref[dz, rows, :].astype(f32) + got_ref[dz, rows, :].astype(f32)).astype(bf16)

    whole = slice(0, ROWS)
    far_a_ref[...] = total(2, slice(0, half))
    far_b_ref[...] = total(2, slice(half, ROWS))
    one_ref[...] = total(1, whole)
    three_ref[...] = total(3, whole)
    near_ref[...] = total(0, whole)


def second_sum_kernel(one_ref, three_ref, up_ref, down_ref, first_ref, last_ref):
    half = ROWS // 2
    first_ref[0:half, :] = (one_ref[0:half, :].astype(f32) + up_ref[...].astype(f32)).astype(bf16)
    first_ref[half:ROWS, :] = one_ref[half:ROWS, :]
    last_ref[0:half, :] = three_ref[0:half, :]
    last_ref[half:ROWS, :] = (three_ref[half:ROWS, :].astype(f32) + down_ref[...].astype(f32)).astype(bf16)


def hidden_kernel(
    part_a, part_b, part_c, dy_ref, hidden_ref, normed_ref, gain_ref, w_ref, wo_ref,
    grad_ref, gain_grad_ref, send_ref, cols_ref, logit_ref,
):
    hidden = hidden_ref[...]
    scale = lax.rsqrt(jnp.mean(hidden * hidden, axis=-1, keepdims=True) + EPS)
    unit = hidden * scale
    total = part_a[...].astype(f32) + part_b[...].astype(f32) + part_c[...].astype(f32)
    tail = total[:, D:XW]
    probs = router_probs(normed_ref[...], w_ref)
    p = tail + pltpu.roll(tail, 128 - 32, 1)
    logit_grad = probs * (p - jnp.sum(p * probs, axis=-1, keepdims=True))
    high = logit_grad.astype(bf16)
    low = (logit_grad - high.astype(f32)).astype(bf16)
    logit_ref[0] = high
    logit_ref[1] = low
    router = w_ref[:, BLK:WW]
    normed_grad = total[:, 0:D] + mm(high, router, NT) + mm(low, router, NT)
    gain_grad_ref[...] = jnp.sum(normed_grad * unit, axis=0, keepdims=True)
    unit_grad = normed_grad * gain_ref[...]
    grad = dy_ref[...].astype(f32) + scale * (unit_grad - unit * jnp.mean(unit_grad * unit, axis=-1, keepdims=True))
    grad_ref[...] = grad
    mix_grad = mm(grad.astype(bf16), wo_ref[...], NT)
    for j in range(OWN):
        cols = slice(j * QW, (j + 1) * QW)
        send_ref[j, :, 0:QW] = mix_grad[:, cols].astype(bf16)
        send_ref[j, :, QW:BLK] = jnp.zeros((ROWS, BLK - QW), bf16)
        cols_ref[j, :, 0:HD] = jnp.zeros((ROWS, HD), bf16)
        cols_ref[j, :, HD:BLK] = grad[:, cols].astype(bf16)


def attend_back_kernel(qkv_ref, log_ref, g_ref, cos_ref, sin_ref, start_ref, dqkv_ref, turn_ref, dk_ref, dv_ref):
    dk_ref[...] = jnp.zeros_like(dk_ref)
    dv_ref[...] = jnp.zeros_like(dv_ref)
    for at in range(0, GROUP, BLK):
        rows = pl.ds(at, BLK)
        keys = at + BLK
        seen = block_mask(start_ref, at, keys)
        k_h = qkv_ref[0:keys, QW : QW + HD]
        v_h = qkv_ref[0:keys, BLK : BLK + HD]
        for r in range(HEADS):
            q_h = qkv_ref[rows, r * HD : (r + 1) * HD] * jnp.asarray(HD**-0.5, bf16)
            g_h = g_ref[rows, r * HD : (r + 1) * HD]
            scores = jnp.where(seen, mm(q_h, k_h, NT), -1e30)
            prob = jnp.exp(scores - log_ref[rows, r : r + 1])
            dv_ref[0:keys, :] += mm(prob.astype(bf16), g_h, TN)
            prob_grad = mm(g_h, v_h, NT)
            delta = jnp.sum(prob_grad * prob, axis=-1, keepdims=True)
            score_grad = (prob * (prob_grad - delta)).astype(bf16)
            turn_ref[rows, r * HD : (r + 1) * HD] = mm(score_grad, k_h) * (HD**-0.5)
            dk_ref[0:keys, :] += mm(score_grad, q_h, TN)
    turn_ref[:, QW : QW + HD] = dk_ref[...]
    for at in range(0, GROUP, BLK):
        rows = pl.ds(at, BLK)
        turned = turn_ref[rows, :]
        turned = turned * twice(cos_ref[rows, :]) - swap_halves(turned) * twice(sin_ref[rows, :])
        dqkv_ref[rows, 0:BLK] = turned.astype(bf16)
        dqkv_ref[rows, BLK : BLK + HD] = dv_ref[rows, :].astype(bf16)
        dqkv_ref[rows, BLK + HD : WW] = jnp.zeros((BLK, WW - BLK - HD), bf16)


def pay_kernel(normed_ref, dqkv_ref, mix_ref, got_ref, n_ref, logit_ref, moe_gain_ref, norm_ref, w_ref, pay_ref):
    left = mm(normed_ref[...], dqkv_ref[:, 0:BLK], TN)
    value = mm(normed_ref[...], dqkv_ref[:, BLK:WW], TN)
    out = mm(mix_ref[...], got_ref[...], TN)
    middle = jnp.concatenate([value, jnp.zeros((D, 128), f32)], axis=1) + out
    router = mm(n_ref[...], logit_ref[0], TN) + mm(n_ref[...], logit_ref[1], TN)
    attn_gain = jnp.sum(left * w_ref[:, 0:BLK].astype(f32), axis=1, keepdims=True)
    attn_gain = attn_gain + jnp.sum(value * w_ref[:, BLK:WW].astype(f32), axis=1, keepdims=True)
    gains = jnp.concatenate([1.0 / norm_ref[...], moe_gain_ref[...], jnp.zeros((126, D), f32)], axis=0)
    gains = jnp.transpose(gains)
    rows = D // DP
    lane = iota((rows, 128), 1)
    attn_gain, moe_gain = attn_gain * gains[:, 0:1], gains[:, 1:2]
    both = jnp.zeros((rows, 128), f32)
    for i in range(DP):
        part = slice(i * rows, (i + 1) * rows)
        both = jnp.where(lane == i, attn_gain[part], jnp.where(lane == DP + i, moe_gain[part], both))
    for i in range(DP):
        part, at = slice(i * rows, (i + 1) * rows), ((i % 4) * 4 + i // 4) * rows
        pay_ref[at : at + rows, 0:BLK] = left[part].astype(bf16)
        pay_ref[at : at + rows, BLK : 2 * BLK] = middle[part].astype(bf16)
        pay_ref[at : at + rows, 2 * BLK : 2 * BLK + 128] = jnp.where(lane >= HD, router[part], both).astype(bf16)


def input_kernel(part_a, part_b, part_c, x_ref, gain_ref, hidden_grad_ref, hidden_ref, out_ref, layer_ref):
    x = x_ref[...].astype(f32)
    scale = lax.rsqrt(jnp.mean(x * x, axis=-1, keepdims=True) + EPS)
    unit = x * scale
    total = part_a[...].astype(f32) + part_b[...].astype(f32) + part_c[...].astype(f32)
    unit_grad = total[:, 0:D] * gain_ref[...]
    out_ref[...] = (
        hidden_grad_ref[...] + scale * (unit_grad - unit * jnp.mean(unit_grad * unit, axis=-1, keepdims=True))
    ).astype(bf16)
    layer_ref[...] = (hidden_ref[...] + total[:, D : 2 * D]).astype(bf16)


def sum_kernel(part_ref, after_ref, sum_ref):
    total = part_ref[0].astype(f32)
    for s in range(1, part_ref.shape[0]):
        total = total + part_ref[s].astype(f32)
    sum_ref[...] = jnp.broadcast_to(total.astype(bf16)[None], sum_ref.shape)


def join_kernel(part_ref, q_ref, k_ref, v_ref, o_ref, router_ref, gain_ref):
    gains = jnp.zeros((D // DP, 128), f32)
    for j in range(OWN):
        part = part_ref[j].astype(f32)
        q_ref[:, j * QW : (j + 1) * QW] = part[:, 0:QW]
        k_ref[:, j * HD : (j + 1) * HD] = part[:, QW:BLK]
        v_ref[:, j * HD : (j + 1) * HD] = part[:, BLK : BLK + HD]
        o_ref[:, j * QW : (j + 1) * QW] = part[:, BLK + HD : 2 * BLK]
        gains = gains + part[:, 2 * BLK : 2 * BLK + 128]
    router_ref[...] = gains[:, HD : HD + EXPERTS]
    gains = jnp.concatenate([gains, jnp.zeros((128 - D // DP, 128), f32)], axis=0)
    gain_ref[...] = jnp.transpose(gains)[0 : 2 * DP]


def sds(shape, dtype):
    return jax.ShapeDtypeStruct(shape, dtype)


def call(kernel, outs, scratch=(), cost=None, **grid):
    return pl.pallas_call(
        kernel,
        out_shape=outs,
        scratch_shapes=list(scratch),
        compiler_params=pltpu.CompilerParams(vmem_limit_bytes=VMEM),
        cost_estimate=cost,
        **grid,
    )


def cost(micros):
    return pl.CostEstimate(flops=int(micros * 1.15e9), bytes_accessed=1024, transcendentals=0)


VM = pl.BlockSpec(memory_space=pltpu.VMEM)
SM = pl.BlockSpec(memory_space=pltpu.SMEM)
ANY = pl.BlockSpec(memory_space=pl.ANY)


def along_z(step):
    return [(i, ((i // 2 + step) % 4) * 2 + i % 2) for i in range(OWN)]


X_GROUPS = [[y, 4 + y, 8 + y, 12 + y] for y in range(4)]
Y_GROUPS = [[4 * x + y for y in range(4)] for x in range(4)]
UP, DOWN, SWAP = along_z(1), along_z(-1), [(i, i ^ 1) for i in range(OWN)]


def move(value, pairs):
    return lax.ppermute(value, "expert", pairs)


def gate(value, *after):
    return pl.pallas_call(
        gate_kernel,
        out_shape=sds(value.shape, value.dtype),
        in_specs=[ANY] * (1 + len(after)),
        out_specs=ANY,
        input_output_aliases={0: 0},
        compiler_params=pltpu.CompilerParams(vmem_limit_bytes=VMEM),
        cost_estimate=cost(0.5),
    )(value, *after)


def ring_rows(value, after=()):
    half = value.shape[0] // 2
    up, down = move(value, UP), move(value, DOWN)
    if after:
        up = gate(up, *after)
    far_a, far_b = move(up[:half], UP), move(down[half:], DOWN)
    return [value, up, down, far_a, far_b]


def swap_rows(mine):
    return mine + [move(piece, SWAP) for piece in mine]


def scatter_rows(keep, send):
    width = keep.shape[2]
    whole, half = sds((ROWS, width), bf16), sds((ROWS // 2, width), bf16)
    near, one, three, far_a, far_b = call(first_sum_kernel, [whole] * 3 + [half] * 2, cost=cost(0.1))(
        keep, move(send, SWAP)
    )
    first, last = call(second_sum_kernel, [whole] * 2, cost=cost(1))(one, three, move(far_a, UP), move(far_b, DOWN))
    return (near, move(first, UP), move(last, DOWN)), far_a


def body(
    tokens, norm_attn, query_weight, key_weight, value_weight, out_weight, norm_moe, router_weight,
    gate_weight, up_weight, down_weight, routes, seq_lengths, out_grad,
):
    own = lax.axis_index("expert").astype(jnp.int32).reshape(1)
    gain_one = norm_attn.reshape(1, D)
    gain_two = norm_moe.reshape(1, D)
    shard_rows = D // DP

    shard, rows = call(
        prep_kernel,
        [sds((DP, shard_rows, WW), bf16), sds((ROWS, XW), bf16)],
        scratch=[pltpu.VMEM((shard_rows, WW), bf16)],
        cost=cost(3),
        in_specs=[SM] + [VM] * 6,
    )(own, query_weight, key_weight, value_weight, router_weight.T, out_grad, routes.T)
    weights = lax.all_to_all(shard, "dp", 0, 0, tiled=True).reshape(D, WW)
    out_full = lax.all_gather(out_weight, "dp", axis=0, tiled=True)
    end_one = seq_lengths[0, 0]
    end_two = end_one + seq_lengths[0, 1]
    place = jnp.arange(GROUP, dtype=jnp.int32)
    start = jnp.where(place >= end_two, end_two, jnp.where(place >= end_one, end_one, 0)).astype(jnp.int32)
    steps = jnp.arange(HD // 2, dtype=f32)
    freq = jnp.exp(steps * (-2.0 * math.log(THETA) / HD))
    angles = (place - start).astype(f32)[:, None] * freq[None, :]
    cos_half, sin_half = jnp.cos(angles), jnp.sin(angles)
    cos_t = jnp.tile(cos_half, (1, 4))
    sin_t = jnp.tile(jnp.concatenate([-sin_half, sin_half], axis=1), (1, 2))
    start = start.reshape(GROUP, 1)
    x_ring = ring_rows(tokens)
    x_ring[1] = gate(x_ring[1], cos_t, sin_t, start, gain_one, gain_two)
    x_pieces = swap_rows(x_ring)
    dy_rows = rows
    dy_up, dy_down = move(dy_rows, UP), move(dy_rows, DOWN)
    dy_ring = [dy_rows, dy_up, dy_down, move(dy_up, UP)]

    part = lambda piece, width, at: pl.BlockSpec(
        (piece.shape[0], width), lambda e: (0, at), pipeline_mode=pl.Buffered(1)
    )
    normed_one, qkv, mix, logs = call(
        attend_kernel,
        [sds((GROUP, D), bf16), sds((GROUP, WW), bf16), sds((OWN, ROWS, BLK), bf16), sds((GROUP, 8), f32)],
        cost=cost(12),
        in_specs=[SM] + [VM] * 15,
    )(own, *x_pieces, weights, gain_one, cos_t, sin_t, start)

    mix_own = lax.all_to_all(gate(mix, dy_ring[2], dy_ring[3]), "expert", 0, 0, tiled=True)
    dy_pieces = swap_rows(dy_ring)
    hidden, normed_two, mix_flat = call(
        out_kernel,
        [sds((ROWS, D), f32), sds((ROWS, D), bf16), sds((ROWS, D), bf16)],
        cost=cost(4),
    )(mix_own, out_full, tokens, gain_two)
    slot_rows, d_slots = call(
        slots_kernel,
        [sds((EXP_DEV, 8, GROUP), jnp.int32), sds((EXP_DEV, SLOTS, D), bf16)],
        scratch=[pltpu.VMEM((TOP, GROUP), f32), pltpu.VMEM((GROUP, D), bf16)],
        cost=cost(6),
        in_specs=[SM] + [VM] * 8,
    )(own, *dy_pieces)
    n_pieces = swap_rows(ring_rows(normed_two, (slot_rows,)))
    mix_flat = gate(mix_flat, n_pieces[1], n_pieces[2])
    mix_all = lax.all_gather(mix_flat, "expert", axis=0, tiled=True)

    whole = lambda *shape: pl.BlockSpec(shape, lambda e: (0,) * len(shape), pipeline_mode=pl.Buffered(1))
    tile = pl.BlockSpec((D, 128), lambda e: (0, 2), pipeline_mode=pl.Buffered(1))
    each = lambda *shape: pl.BlockSpec((1,) + shape, lambda e: (e, 0, 0))
    grads, hg, hu, inner, gates = call(
        expert_kernel,
        [
            sds((EXP_DEV, 3, D, FFE), bf16), sds((EXP_DEV, SLOTS, FFE), bf16), sds((EXP_DEV, SLOTS, FFE), bf16), sds((EXP_DEV, SLOTS, FFE), bf16),
            sds((EXP_DEV, SLOTS, 1), f32),
        ],
        scratch=[
            pltpu.VMEM((128, GROUP), f32), pltpu.VMEM((SLOTS, D), bf16), pltpu.VMEM((GROUP, D), bf16),
        ],
        cost=cost(28),
        grid=(EXP_DEV,),
        in_specs=[
            SM, *[whole(*p.shape) for p in n_pieces], tile, each(SLOTS, D), each(8, GROUP),
            each(D, FFE), each(D, FFE), each(FFE, D),
        ],
        out_specs=[
            pl.BlockSpec((1, 3, D, FFE), lambda e: (e, 0, 0, 0)),
            each(SLOTS, FFE), each(SLOTS, FFE), each(SLOTS, FFE), each(SLOTS, 1),
        ],
    )(own, *n_pieces, weights, d_slots, slot_rows, gate_weight, up_weight, down_weight)

    grad_sums = lax.psum(gate(grads, mix_all).reshape(EXP_DEV * 3 * D, FFE), "dp")

    dx_keep, dx_send, gated = call(
        return_kernel,
        [sds((PAIRS, ROWS, XW), bf16)] * 2 + [sds((EXP_DEV, SLOTS, D), bf16)],
        scratch=[pltpu.VMEM((EXP_DEV, SLOTS, D), bf16), pltpu.VMEM((EXP_DEV, SLOTS, 128), bf16)],
        cost=cost(1),
        grid=(EXP_DEV,),
        in_specs=[
            SM, each(SLOTS, FFE), each(SLOTS, FFE), each(SLOTS, FFE), each(SLOTS, 1), each(SLOTS, D),
            whole(EXP_DEV, 8, GROUP), each(D, FFE), each(D, FFE), each(FFE, D),
        ],
        out_specs=[whole(PAIRS, ROWS, XW)] * 2 + [each(SLOTS, D)],
    )(own, hg, hu, inner, gates, d_slots, slot_rows, gate_weight, up_weight, down_weight)

    dx_parts, _ = scatter_rows(dx_keep, dx_send)
    hidden_grad, moe_gain, send, cols, logit_grads = call(
        hidden_kernel,
        [sds((ROWS, D), f32), sds((1, D), f32), sds((OWN, ROWS, BLK), bf16), sds((OWN, ROWS, BLK), bf16),
            sds((2, ROWS, 128), bf16)],
        cost=cost(1),
    )(*dx_parts, out_grad, hidden, normed_two, gain_two, weights, out_full)
    mix_grad = lax.all_to_all(send, "expert", 0, 0, tiled=True).reshape(GROUP, BLK)
    got = lax.all_to_all(cols, "expert", 0, 0, tiled=True).reshape(GROUP, BLK)
    dqkv = call(
        attend_back_kernel,
        sds((GROUP, WW), bf16),
        scratch=[pltpu.VMEM((GROUP, BLK), f32), pltpu.VMEM((GROUP, HD), f32), pltpu.VMEM((GROUP, HD), f32)],
        cost=cost(12),
    )(qkv, logs, mix_grad, cos_t, sin_t, start)
    pay = call(pay_kernel, sds((D, 640), bf16), cost=cost(1))(
        normed_one, dqkv, mix_all, got, normed_two, logit_grads, moe_gain, gain_one, weights
    )
    pay_parts = lax.all_to_all(pay.reshape(4, D // 4, 640), "dp", 0, 0, tiled=True, axis_index_groups=Y_GROUPS)
    rows_keep, rows_send = call(
        tokens_kernel, [sds((PAIRS, ROWS, 2 * D), bf16)] * 2, cost=cost(0.1), in_specs=[SM] + [VM] * 4 + [ANY]
    )(own, gated, slot_rows, dqkv, weights, pay)
    rows_parts, rows_first = scatter_rows(rows_keep, rows_send)
    pay_line = call(
        sum_kernel, sds((1, D // 4, 640), bf16), cost=cost(0.1), in_specs=[VM, ANY]
    )(pay_parts, rows_first)
    pay_parts = lax.all_to_all(
        pay_line.reshape(4, shard_rows, 640), "dp", 0, 0, tiled=True, axis_index_groups=X_GROUPS
    )
    pay_own = call(
        sum_kernel, sds((OWN, shard_rows, 640), bf16), cost=cost(0.1), in_specs=[VM, ANY]
    )(pay_parts, pay_line)
    pay_all = lax.all_to_all(pay_own, "expert", 0, 0, tiled=True)
    query_total, key_total, value_total, out_total, router_total, gains = call(
        join_kernel,
        [sds((shard_rows, w), f32) for w in (D, KVH * HD, KVH * HD, D, EXPERTS)] + [sds((2 * DP, 128), f32)],
        cost=cost(0.02),
    )(pay_all)
    gain_attn = gains[0:DP, :shard_rows].reshape(D)
    gain_moe = gains[DP:, :shard_rows].reshape(D)
    input_grad, layer_out = call(input_kernel, [sds((ROWS, D), bf16)] * 2, cost=cost(1))(
        *rows_parts, tokens, gain_one, hidden_grad, hidden
    )
    gate_total, up_total, down_total = call(
        widen_kernel,
        [sds((EXP_DEV, D, FFE), f32), sds((EXP_DEV, D, FFE), f32), sds((EXP_DEV, FFE, D), f32)],
        scratch=[
            pltpu.VMEM((6, D // 2, FFE), bf16), pltpu.VMEM((6, D // 2, FFE), f32),
            pltpu.SemaphoreType.DMA((6, 3)), pltpu.SemaphoreType.DMA((6, 3)),
        ],
        cost=cost(12),
        in_specs=[ANY],
        out_specs=[ANY] * 3,
    )(grad_sums.reshape(EXP_DEV, 3, D, FFE))
    return (
        layer_out, input_grad, gain_attn, query_total, key_total, value_total, out_total, gain_moe, router_total,
        gate_total, up_total, down_total,
    )


def solution(mesh):
    both, dp, expert = P(("dp", "expert"), None), P("dp", None), P("expert", None, None)
    return jax.shard_map(
        body,
        mesh=mesh,
        in_specs=(both, P(), dp, dp, dp, dp, P(), dp, expert, expert, expert, both, dp, both),
        out_specs=(both, both, P(), dp, dp, dp, dp, P(), dp, expert, expert, expert),
        check_vma=False,
    )
```
